32 devices in a mesh: energy: 8 (over z, x), mom: 4 (over y, core).
Axes of the slice: x: 2, y: 2, z: 4, core: 2. Of those that a mesh axis runs over, the one named last changes fastest.
Arguments:
- green_less: float32 [4, 8, 8, 64, 128], P('mom', 'energy'), may hold values from -6 to 6
- couplings: bfloat16 [32, 3, 64, 64], replicated, may hold values from -0.75 to 0.75
- pair_atoms: int32 [8, 2], replicated, may hold values from 0 to 31
- shift_idx: int32 [3], replicated, may hold values from 1 to 4, as said below
- weights: float32 [2, 3, 4], replicated, may hold values from 0.05 to 1
Outputs:
- sigma_less: float32 [4, 8, 8, 64, 128], P('mom', 'energy')
The draws below stay inside these ranges and needn't reach their ends.
Inputs may be any that keep to these rules, and one draw needn't show every extreme that they name: `shift_idx`: one mode's shift is exactly 4 and another's is exactly 1.
All inputs are finite; a program needn't handle non-finite values.
Results may differ from the reference program's by a relative error of at most 0.0003.
Values sent between devices are 32-bit elements; how exact they have to be, the bound alone decides.
A program may use at most 64 MiB of HBM per device.

```python
import math
import jax
import jax.numpy as jnp
from jax import lax

B = 64
NMODE = 3
SHIFT_MAX = 4
NATOM = 32
NK = 4
NE = 8
P_SIZE = 8


def draw_shift_idx(key, part):
    first_key, second_key = jax.random.split(key)
    values = jax.random.randint(first_key, (NMODE,), 1, SHIFT_MAX + 1)
    ranking = jax.random.permutation(second_key, NMODE)
    values = values.at[ranking[0]].set(SHIFT_MAX)
    values = values.at[ranking[1]].set(1)
    return values.astype(jnp.int32)


def plant(result, stream_key, smallest, top_value):
    longest = result.shape.index(max(result.shape))
    spots = []
    for shift in (0, 1):
        where = [jax.random.randint(jax.random.fold_in(stream_key, axis), (), 0, length) for axis, length in enumerate(result.shape)]
        where[longest] = (where[longest] + shift) % result.shape[longest]
        spots.append(tuple(where))
    return result.at[spots[0]].set(smallest).at[spots[1]].set(top_value)


def block_levels(rng, extent, pieces, least, high):
    loudness, own = 1.0, jax.random.fold_in(rng, 6)
    for dim, shards_of in pieces:
        steps = jnp.exp(jax.random.uniform(jax.random.fold_in(own, dim), (shards_of,), jnp.float32, least / len(pieces), high / len(pieces)))
        loudness = loudness * jnp.repeat(steps, extent[dim] // shards_of).reshape([-1 if axis == dim else 1 for axis in range(len(extent))])
    return loudness


def normal_values(rng, shape, scale, limit, shards=(), kind=jnp.bfloat16):
    loudness = block_levels(rng, shape, shards, -0.22, 0.18) if shards else 1.0
    drawn = jax.random.normal(rng, shape, jnp.float32) * scale * loudness
    return jnp.minimum(jnp.maximum(drawn, -limit), limit).astype(kind)


def setup_inputs(seed: int = 0) -> dict:
    keys = jax.random.split(jax.random.key(seed), 6)
    return {
        "green_less": normal_values(keys[0], (NK, NE, P_SIZE, B, 2 * B), 1.0, 6.0, ((0, 4), (1, 8)), jnp.float32),
        "couplings": normal_values(keys[1], (NATOM, NMODE, B, B), B ** -0.5, 0.75),
        "pair_atoms": plant(jax.random.randint(keys[2], (P_SIZE, 2), 0, NATOM), jax.random.fold_in(keys[2], 1), 0, NATOM - 1).astype(jnp.int32),
        "shift_idx": draw_shift_idx(jax.random.fold_in(keys[5], 71), 0),
        "weights": jnp.clip(jnp.exp(jax.random.uniform(keys[4], (2, NMODE, NK), jnp.float32, math.log(0.05), math.log(1.0))), 0.05, 1.0),
    }


precise = lax.Precision.HIGHEST


def circulant(weights):
    moments = weights.shape[2]
    target_ids = jnp.arange(moments, dtype=jnp.int32)[:, None]
    source_ids = jnp.arange(moments, dtype=jnp.int32)[None, :]
    offset = (target_ids - source_ids) % moments
    selector = (offset[:, :, None] == jnp.arange(moments, dtype=jnp.int32)[None, None, :]).astype(jnp.float32)
    return jnp.einsum("slm,kjm->slkj", weights, selector, precision=precise)


def pair_sigma(green_pair, left_coupling, right_coupling, mixing, shift_idx):
    moments = green_pair.shape[0]
    energies = green_pair.shape[1]
    orbitals = green_pair.shape[2]
    padded = jnp.pad(green_pair, ((0, 0), (SHIFT_MAX, SHIFT_MAX), (0, 0), (0, 0)))
    summed = jnp.zeros(green_pair.shape, jnp.float32)
    for mode_index in range(NMODE):
        shift_now = shift_idx[mode_index]
        below_shift = lax.dynamic_slice_in_dim(padded, (SHIFT_MAX - shift_now).astype(jnp.int32), energies, 1)
        above_shift = lax.dynamic_slice_in_dim(padded, (SHIFT_MAX + shift_now).astype(jnp.int32), energies, 1)
        mixed = jnp.einsum("kj,jeac->keac", mixing[0, mode_index], below_shift, precision=precise)
        mixed = mixed + jnp.einsum("kj,jeac->keac", mixing[1, mode_index], above_shift, precision=precise)
        left_product = jnp.einsum("ab,kebc->keac", left_coupling[mode_index], mixed, precision=precise)
        halves = left_product.reshape(moments, energies, orbitals, 2, orbitals)
        right_product = jnp.einsum("keaqc,dc->keaqd", halves, right_coupling[mode_index], precision=precise)
        summed = summed + right_product.reshape(green_pair.shape)
    return summed


def reference(green_less, couplings, pair_atoms, shift_idx, weights):
    mixing = circulant(weights)
    coupling_table = couplings.astype(jnp.float32)

    def one_pair(pair_index):
        green_pair = lax.dynamic_index_in_dim(green_less, pair_index, 2, keepdims=False)
        left_coupling = coupling_table[pair_atoms[pair_index, 0]]
        right_coupling = coupling_table[pair_atoms[pair_index, 1]]
        return pair_sigma(green_pair, left_coupling, right_coupling, mixing, shift_idx)

    stacked = lax.map(one_pair, jnp.arange(P_SIZE, dtype=jnp.int32))
    return jnp.moveaxis(stacked, 0, 2)
```

```python
import functools

import jax
import jax.numpy as jnp
from jax import lax
from jax.experimental import pallas as pl
from jax.experimental.pallas import tpu as pltpu
from jax.sharding import PartitionSpec as P

HALVES = 2
SHIFT_MAX = 4
MESH = pl.DeviceIdType.MESH


def split(value):
    high = value.astype(jnp.bfloat16)
    return high, (value - high.astype(jnp.float32)).astype(jnp.bfloat16)


def left_lanes(shape):
    return lax.broadcasted_iota(jnp.int32, shape, len(shape) - 1) < shape[-1] // 2


def iota(shape, axis):
    return lax.broadcasted_iota(jnp.int32, shape, axis)


def kernel(
    sizes,
    green_hbm, couplings_hbm, pair_atoms, shift_idx, weights,
    out_ref,
    green, couplings, packed, held, result, landed, left_table, right_table,
    load_sem, in_send, in_recv, side_send, side_recv, out_send, out_recv,
):
    moms, energies, modes, orbitals, group = sizes
    lanes = 2 * orbitals
    rows = orbitals // 2
    cores = moms // HALVES
    here = lax.axis_index("energy")
    mom = lax.axis_index("mom")
    half, core = mom // cores, mom % cores

    def device(at, half_at, core_at):
        return (at, half_at * cores + core_at)

    def around(base, step, size):
        return lax.rem(base + step, size)

    barrier = pltpu.get_barrier_semaphore()
    for turn in range(HALVES):
        for step in range(1 if turn == 0 else 0, energies):
            pl.semaphore_signal(
                barrier, inc=1,
                device_id=device(around(here, step, energies), around(half, turn, HALVES), core),
                device_id_type=MESH,
            )
    for turn in range(1, cores):
        pl.semaphore_signal(
            barrier, inc=1, device_id=device(here, half, around(core, turn, cores)), device_id_type=MESH
        )

    load_green = pltpu.make_async_copy(green_hbm, green, load_sem.at[0])
    load_green.start()
    load_couplings = pltpu.make_async_copy(couplings_hbm, couplings, load_sem.at[1])
    load_couplings.start()

    edge = jnp.zeros((SHIFT_MAX, rows, lanes), jnp.float32)
    for source in range(moms):
        held[source, pl.ds(0, SHIFT_MAX)] = edge
        held[source, pl.ds(SHIFT_MAX + energies, SHIFT_MAX)] = edge

    load_green.wait()
    mask = left_lanes((rows, lanes))
    for pair in range(energies):
        top = green[0, 0, pair, pl.ds(0, rows), :]
        bottom = green[0, 0, pair, pl.ds(rows, rows), :]
        packed[0, pair] = jnp.where(mask, top, pltpu.roll(bottom, orbitals, 1))
        packed[1, pair] = jnp.where(mask, pltpu.roll(top, orbitals, 1), bottom)

    pl.semaphore_wait(barrier, HALVES * energies - 1 + cores - 1)

    def send_in(turn, step):
        to_half, to = around(half, turn, HALVES), around(here, step, energies)
        return pltpu.make_async_remote_copy(
            src_ref=packed.at[to_half, to],
            dst_ref=held.at[mom, SHIFT_MAX + here],
            send_sem=in_send.at[turn, step],
            recv_sem=in_recv.at[turn, step],
            device_id=device(to, to_half, core),
            device_id_type=MESH,
        )

    def send_side(turn, step, side):
        source = around(half, turn, HALVES) * cores + core
        slot = SHIFT_MAX + around(here, energies - step, energies)
        return pltpu.make_async_remote_copy(
            src_ref=held.at[source, slot],
            dst_ref=held.at[source, slot],
            send_sem=side_send.at[side, turn, step],
            recv_sem=side_recv.at[side, turn, step],
            device_id=device(here, half, around(core, side, cores)),
            device_id_type=MESH,
        )

    far_first = sorted(range(energies), key=lambda step: -min(step, energies - step))
    slots = [(turn, step) for step in far_first for turn in range(HALVES)]
    near_first = slots[::-1]
    remote = [slot for slot in slots if slot != (0, 0)]
    for turn, step in remote:
        send_in(turn, step).start()

    held[mom, SHIFT_MAX + here] = packed[half, here]

    load_couplings.wait()
    atom_a = pair_atoms[here, 0]
    atom_b = pair_atoms[here, 1]
    pick_same = (iota((orbitals, lanes), 0) == iota((orbitals, lanes), 1) % orbitals).astype(jnp.bfloat16)
    pick_other = (
        iota((orbitals, lanes), 0) == (iota((orbitals, lanes), 1) + rows) % orbitals
    ).astype(jnp.bfloat16)
    upper = iota((orbitals, lanes), 0) < rows
    same_block = (iota((lanes, lanes), 0) < orbitals) == (iota((lanes, lanes), 1) < orbitals)
    for mode in range(modes):
        left = couplings[atom_a, mode]
        right = couplings[atom_b, mode]
        left_same = jnp.dot(left, pick_same, preferred_element_type=jnp.float32)
        left_other = jnp.dot(left, pick_other, preferred_element_type=jnp.float32)
        left_table[:, pl.ds(mode * lanes, lanes)] = jnp.where(upper, left_same, left_other).astype(jnp.bfloat16)
        wide = jnp.dot(right, pick_same, preferred_element_type=jnp.float32).astype(jnp.bfloat16)
        tall = jnp.concatenate([wide, wide], axis=0)
        diagonal = jnp.where(same_block, tall.astype(jnp.float32), 0.0).astype(jnp.bfloat16)
        right_table[mode] = jnp.concatenate([diagonal, diagonal], axis=1)

    for turn, step in near_first:
        if (turn, step) != (0, 0):
            send_in(turn, step).wait_recv()
        for side in range(1, cores):
            send_side(turn, step, side).start()
    for turn, step in near_first:
        for side in range(1, cores):
            send_side(turn, step, side).wait_recv()

    def send_out(to_half, to):
        turn = lax.rem(to_half - half + HALVES, HALVES)
        step = lax.rem(to - here + energies, energies)
        return pltpu.make_async_remote_copy(
            src_ref=result.at[to_half, to],
            dst_ref=landed.at[half, here],
            send_sem=out_send.at[turn, step],
            recv_sem=out_recv.at[turn, step],
            device_id=device(to, to_half, core),
            device_id_type=MESH,
        )

    def one_group(index, carry):
        first = lax.rem(here // group + 1 + index, energies // group) * group
        sums = [[] for _ in range(modes)]
        for member in range(group):
            energy = first + member
            for mode in range(modes):
                shift = shift_idx[mode]
                totals = [None] * HALVES
                for offset in range(moms):
                    source = lax.rem(core - offset + moms, moms)
                    for sign, slot in ((0, energy - shift), (1, energy + shift)):
                        value = held[source, SHIFT_MAX + slot]
                        for target in range(HALVES):
                            term = weights[sign, mode, (target * cores + offset) % moms] * value
                            totals[target] = term if totals[target] is None else totals[target] + term
                sums[mode].extend(totals)
        rights = []
        for mode in range(modes):
            high, low = split(jnp.concatenate(sums[mode], axis=0))
            rights.append(
                lax.dot_general(
                    jnp.concatenate([high, low], axis=1), right_table[mode],
                    (((1,), (1,)), ((), ())), preferred_element_type=jnp.float32,
                )
            )
        for member in range(group):
            columns = []
            for target in range(HALVES):
                start = (member * HALVES + target) * rows
                stack = []
                for mode in range(modes):
                    block = rights[mode][start:start + rows]
                    high, low = split(jnp.concatenate([block, pltpu.roll(block, orbitals, 1)], axis=0))
                    stack += [high, low]
                columns.append(jnp.concatenate(stack, axis=0))
            product = jnp.dot(
                left_table[...], jnp.concatenate(columns, axis=1), preferred_element_type=jnp.float32
            )
            energy = first + member
            for target in range(HALVES):
                both = product[:, target * lanes:(target + 1) * lanes]
                result[target, energy] = jnp.where(mask, both[:rows], both[rows:])
                own = jnp.logical_and(energy == here, half == target)

                @pl.when(jnp.logical_not(own))
                def _():
                    send_out(target, energy).start()

        return carry

    lax.fori_loop(0, energies // group, one_group, 0)
    landed[half, here] = result[half, here]

    for step in reversed(far_first):
        for turn in range(HALVES):
            if (turn, step) != (0, 0):
                send_out(around(half, turn, HALVES), around(here, step, energies)).wait_recv()
        pair = around(here, energies - step, energies)
        real, imag = landed[0, pair], landed[1, pair]
        out_ref[0, 0, pair, pl.ds(0, rows), :] = jnp.where(mask, real, pltpu.roll(imag, orbitals, 1))
        out_ref[0, 0, pair, pl.ds(rows, rows), :] = jnp.where(mask, pltpu.roll(real, orbitals, 1), imag)

    for turn, step in slots:
        if (turn, step) != (0, 0):
            send_in(turn, step).wait_send()
            send_out(around(half, turn, HALVES), around(here, step, energies)).wait_send()
        for side in range(1, cores):
            send_side(turn, step, side).wait_send()


def on_device(moms, energies, green_less, couplings, pair_atoms, shift_idx, weights):
    modes, orbitals = couplings.shape[1], couplings.shape[2]
    lanes, rows, cores = 2 * orbitals, orbitals // 2, moms // HALVES
    group = next(size for size in (4, 2, 1) if energies % size == 0)
    smem = pl.BlockSpec(memory_space=pltpu.SMEM)
    hbm = pl.BlockSpec(memory_space=pl.ANY)
    dma = pltpu.SemaphoreType.DMA
    return pl.pallas_call(
        functools.partial(kernel, (moms, energies, modes, orbitals, group)),
        out_shape=jax.ShapeDtypeStruct(green_less.shape, jnp.float32),
        in_specs=[hbm, hbm, smem, smem, smem],
        out_specs=pl.BlockSpec(memory_space=pltpu.VMEM),
        scratch_shapes=[
            pltpu.VMEM(green_less.shape, jnp.float32),
            pltpu.VMEM(couplings.shape, jnp.bfloat16),
            pltpu.VMEM((HALVES, energies, rows, lanes), jnp.float32),
            pltpu.VMEM((moms, energies + 2 * SHIFT_MAX, rows, lanes), jnp.float32),
            pltpu.VMEM((HALVES, energies, rows, lanes), jnp.float32),
            pltpu.VMEM((HALVES, energies, rows, lanes), jnp.float32),
            pltpu.VMEM((orbitals, modes * lanes), jnp.bfloat16),
            pltpu.VMEM((modes, lanes, 2 * lanes), jnp.bfloat16),
            dma((2,)),
            dma((HALVES, energies)),
            dma((HALVES, energies)),
            dma((cores, HALVES, energies)),
            dma((cores, HALVES, energies)),
            dma((HALVES, energies)),
            dma((HALVES, energies)),
        ],
        compiler_params=pltpu.CompilerParams(
            collective_id=0, has_side_effects=True, vmem_limit_bytes=40 * 2**20
        ),
    )(green_less, couplings, pair_atoms, shift_idx, weights)


def solution(mesh):
    spec = P("mom", "energy", None, None, None)
    return jax.shard_map(
        functools.partial(on_device, mesh.shape["mom"], mesh.shape["energy"]),
        mesh=mesh,
        in_specs=(spec, P(), P(), P(), P()),
        out_specs=spec,
        check_vma=False,
    )
```

```python
import functools

import jax
import jax.numpy as jnp
from jax import lax
from jax.experimental import pallas as pl
from jax.experimental.pallas import tpu as pltpu
from jax.sharding import PartitionSpec as P

HALVES = 2
SHIFT_MAX = 4
MESH = pl.DeviceIdType.MESH


def split(value):
    high = value.astype(jnp.bfloat16)
    return high, (value - high.astype(jnp.float32)).astype(jnp.bfloat16)


def left_lanes(shape):
    return lax.broadcasted_iota(jnp.int32, shape, len(shape) - 1) < shape[-1] // 2


def iota(shape, axis):
    return lax.broadcasted_iota(jnp.int32, shape, axis)


def kernel(
    sizes,
    green_hbm, couplings_hbm, pair_atoms_hbm, shift_idx_hbm, weights_hbm,
    out_ref,
    green, couplings, pair_atoms, shift_idx, weights, packed, held, result, landed, left_table, right_table,
    load_sem, in_send, in_recv, side_send, side_recv, out_send, out_recv,
):
    moms, energies, modes, orbitals, group = sizes
    lanes = 2 * orbitals
    rows = orbitals // 2
    cores = moms // HALVES
    here = lax.axis_index("energy")
    mom = lax.axis_index("mom")
    half, core = mom // cores, mom % cores

    def device(at, half_at, core_at):
        return (at, half_at * cores + core_at)

    def around(base, step, size):
        return lax.rem(base + step, size)

    barrier = pltpu.get_barrier_semaphore()
    for turn in range(HALVES):
        for step in range(1 if turn == 0 else 0, energies):
            pl.semaphore_signal(
                barrier, inc=1,
                device_id=device(around(here, step, energies), around(half, turn, HALVES), core),
                device_id_type=MESH,
            )
    for turn in range(1, cores):
        pl.semaphore_signal(
            barrier, inc=1, device_id=device(here, half, around(core, turn, cores)), device_id_type=MESH
        )

    load_green = pltpu.make_async_copy(green_hbm, green, load_sem.at[0])
    load_green.start()
    load_couplings = pltpu.make_async_copy(couplings_hbm, couplings, load_sem.at[1])
    load_couplings.start()
    load_small = [
        pltpu.make_async_copy(pair_atoms_hbm, pair_atoms, load_sem.at[2]),
        pltpu.make_async_copy(shift_idx_hbm, shift_idx, load_sem.at[3]),
        pltpu.make_async_copy(weights_hbm, weights, load_sem.at[4]),
    ]
    for load in load_small:
        load.start()

    edge = jnp.zeros((SHIFT_MAX, rows, lanes), jnp.float32)
    for source in range(moms):
        held[source, pl.ds(0, SHIFT_MAX)] = edge
        held[source, pl.ds(SHIFT_MAX + energies, SHIFT_MAX)] = edge

    load_green.wait()
    mask = left_lanes((rows, lanes))
    for pair in range(energies):
        top = green[0, 0, pair, pl.ds(0, rows), :]
        bottom = green[0, 0, pair, pl.ds(rows, rows), :]
        packed[0, pair] = jnp.where(mask, top, pltpu.roll(bottom, orbitals, 1))
        packed[1, pair] = jnp.where(mask, pltpu.roll(top, orbitals, 1), bottom)

    pl.semaphore_wait(barrier, HALVES * energies - 1 + cores - 1)

    def send_in(turn, step):
        to_half, to = around(half, turn, HALVES), around(here, step, energies)
        return pltpu.make_async_remote_copy(
            src_ref=packed.at[to_half, to],
            dst_ref=held.at[mom, SHIFT_MAX + here],
            send_sem=in_send.at[turn, step],
            recv_sem=in_recv.at[turn, step],
            device_id=device(to, to_half, core),
            device_id_type=MESH,
        )

    def send_side(turn, step, side):
        source = around(half, turn, HALVES) * cores + core
        slot = SHIFT_MAX + around(here, energies - step, energies)
        return pltpu.make_async_remote_copy(
            src_ref=held.at[source, slot],
            dst_ref=held.at[source, slot],
            send_sem=side_send.at[side, turn, step],
            recv_sem=side_recv.at[side, turn, step],
            device_id=device(here, half, around(core, side, cores)),
            device_id_type=MESH,
        )

    far_first = sorted(range(energies), key=lambda step: -min(step, energies - step))
    slots = [(turn, step) for step in far_first for turn in range(HALVES)]
    near_first = slots[::-1]
    remote = [slot for slot in slots if slot != (0, 0)]
    for turn, step in remote:
        send_in(turn, step).start()

    held[mom, SHIFT_MAX + here] = packed[half, here]

    load_couplings.wait()
    for load in load_small:
        load.wait()
    atom_a = pair_atoms[0, here]
    atom_b = pair_atoms[1, here]
    pick_same = (iota((orbitals, lanes), 0) == iota((orbitals, lanes), 1) % orbitals).astype(jnp.bfloat16)
    pick_other = (
        iota((orbitals, lanes), 0) == (iota((orbitals, lanes), 1) + rows) % orbitals
    ).astype(jnp.bfloat16)
    upper = iota((orbitals, lanes), 0) < rows
    same_block = (iota((lanes, lanes), 0) < orbitals) == (iota((lanes, lanes), 1) < orbitals)
    for mode in range(modes):
        left = couplings[atom_a, mode]
        right = couplings[atom_b, mode]
        left_same = jnp.dot(left, pick_same, preferred_element_type=jnp.float32)
        left_other = jnp.dot(left, pick_other, preferred_element_type=jnp.float32)
        left_table[:, pl.ds(mode * lanes, lanes)] = jnp.where(upper, left_same, left_other).astype(jnp.bfloat16)
        wide = jnp.dot(right, pick_same, preferred_element_type=jnp.float32).astype(jnp.bfloat16)
        tall = jnp.concatenate([wide, wide], axis=0)
        diagonal = jnp.where(same_block, tall.astype(jnp.float32), 0.0).astype(jnp.bfloat16)
        right_table[mode] = jnp.concatenate([diagonal, diagonal], axis=1)

    for turn, step in near_first:
        if (turn, step) != (0, 0):
            send_in(turn, step).wait_recv()
        for side in range(1, cores):
            send_side(turn, step, side).start()
    for turn, step in near_first:
        for side in range(1, cores):
            send_side(turn, step, side).wait_recv()

    def send_out(to_half, to):
        turn = lax.rem(to_half - half + HALVES, HALVES)
        step = lax.rem(to - here + energies, energies)
        return pltpu.make_async_remote_copy(
            src_ref=result.at[to_half, to],
            dst_ref=landed.at[half, here],
            send_sem=out_send.at[turn, step],
            recv_sem=out_recv.at[turn, step],
            device_id=device(to, to_half, core),
            device_id_type=MESH,
        )

    def one_group(index, carry):
        first = lax.rem(here // group + 1 + index, energies // group) * group
        sums = [[] for _ in range(modes)]
        for member in range(group):
            energy = first + member
            for mode in range(modes):
                shift = shift_idx[mode]
                totals = [None] * HALVES
                for offset in range(moms):
                    source = lax.rem(core - offset + moms, moms)
                    for sign, slot in ((0, energy - shift), (1, energy + shift)):
                        value = held[source, SHIFT_MAX + slot]
                        for target in range(HALVES):
                            term = weights[mode, sign, (target * cores + offset) % moms] * value
                            totals[target] = term if totals[target] is None else totals[target] + term
                sums[mode].extend(totals)
        rights = []
        for mode in range(modes):
            high, low = split(jnp.concatenate(sums[mode], axis=0))
            rights.append(
                lax.dot_general(
                    jnp.concatenate([high, low], axis=1), right_table[mode],
                    (((1,), (1,)), ((), ())), preferred_element_type=jnp.float32,
                )
            )
        for member in range(group):
            columns = []
            for target in range(HALVES):
                start = (member * HALVES + target) * rows
                stack = []
                for mode in range(modes):
                    block = rights[mode][start:start + rows]
                    high, low = split(jnp.concatenate([block, pltpu.roll(block, orbitals, 1)], axis=0))
                    stack += [high, low]
                columns.append(jnp.concatenate(stack, axis=0))
            product = jnp.dot(
                left_table[...], jnp.concatenate(columns, axis=1), preferred_element_type=jnp.float32
            )
            energy = first + member
            for target in range(HALVES):
                both = product[:, target * lanes:(target + 1) * lanes]
                result[target, energy] = jnp.where(mask, both[:rows], both[rows:])
                own = jnp.logical_and(energy == here, half == target)

                @pl.when(jnp.logical_not(own))
                def _():
                    send_out(target, energy).start()

        return carry

    lax.fori_loop(0, energies // group, one_group, 0)
    landed[half, here] = result[half, here]

    for step in reversed(far_first):
        for turn in range(HALVES):
            if (turn, step) != (0, 0):
                send_out(around(half, turn, HALVES), around(here, step, energies)).wait_recv()
        pair = around(here, energies - step, energies)
        real, imag = landed[0, pair], landed[1, pair]
        out_ref[0, 0, pair, pl.ds(0, rows), :] = jnp.where(mask, real, pltpu.roll(imag, orbitals, 1))
        out_ref[0, 0, pair, pl.ds(rows, rows), :] = jnp.where(mask, pltpu.roll(real, orbitals, 1), imag)

    for turn, step in slots:
        if (turn, step) != (0, 0):
            send_in(turn, step).wait_send()
            send_out(around(half, turn, HALVES), around(here, step, energies)).wait_send()
        for side in range(1, cores):
            send_side(turn, step, side).wait_send()


def on_device(moms, energies, green_less, couplings, pair_atoms, shift_idx, weights):
    modes, orbitals = couplings.shape[1], couplings.shape[2]
    lanes, rows, cores = 2 * orbitals, orbitals // 2, moms // HALVES
    group = next(size for size in (4, 2, 1) if energies % size == 0)
    atoms_first = pair_atoms.T
    modes_first = weights.transpose(1, 0, 2)
    hbm = pl.BlockSpec(memory_space=pl.ANY)
    dma = pltpu.SemaphoreType.DMA
    return pl.pallas_call(
        functools.partial(kernel, (moms, energies, modes, orbitals, group)),
        out_shape=jax.ShapeDtypeStruct(green_less.shape, jnp.float32),
        in_specs=[hbm] * 5,
        out_specs=pl.BlockSpec(memory_space=pltpu.VMEM),
        scratch_shapes=[
            pltpu.VMEM(green_less.shape, jnp.float32),
            pltpu.VMEM(couplings.shape, jnp.bfloat16),
            pltpu.SMEM(atoms_first.shape, jnp.int32),
            pltpu.SMEM(shift_idx.shape, jnp.int32),
            pltpu.SMEM(modes_first.shape, jnp.float32),
            pltpu.VMEM((HALVES, energies, rows, lanes), jnp.float32),
            pltpu.VMEM((moms, energies + 2 * SHIFT_MAX, rows, lanes), jnp.float32),
            pltpu.VMEM((HALVES, energies, rows, lanes), jnp.float32),
            pltpu.VMEM((HALVES, energies, rows, lanes), jnp.float32),
            pltpu.VMEM((orbitals, modes * lanes), jnp.bfloat16),
            pltpu.VMEM((modes, lanes, 2 * lanes), jnp.bfloat16),
            dma((5,)),
            dma((HALVES, energies)),
            dma((HALVES, energies)),
            dma((cores, HALVES, energies)),
            dma((cores, HALVES, energies)),
            dma((HALVES, energies)),
            dma((HALVES, energies)),
        ],
        compiler_params=pltpu.CompilerParams(
            collective_id=0, has_side_effects=True, vmem_limit_bytes=60 * 2**20
        ),
    )(green_less, couplings, atoms_first, shift_idx, modes_first)


def solution(mesh):
    spec = P("mom", "energy", None, None, None)
    return jax.shard_map(
        functools.partial(on_device, mesh.shape["mom"], mesh.shape["energy"]),
        mesh=mesh,
        in_specs=(spec, P(), P(), P(), P()),
        out_specs=spec,
        check_vma=False,
    )
```

```python
import functools

import jax
import jax.numpy as jnp
from jax import lax
from jax.experimental import pallas as pl
from jax.experimental.pallas import tpu as pltpu
from jax.sharding import PartitionSpec as P

HALVES = 2
SHIFT_MAX = 4
MESH = pl.DeviceIdType.MESH


def split(value):
    high = value.astype(jnp.bfloat16)
    return high, (value - high.astype(jnp.float32)).astype(jnp.bfloat16)


def left_lanes(shape):
    return lax.broadcasted_iota(jnp.int32, shape, len(shape) - 1) < shape[-1] // 2


def iota(shape, axis):
    return lax.broadcasted_iota(jnp.int32, shape, axis)


def kernel(
    sizes,
    green_hbm, couplings_hbm, pair_atoms_hbm, shift_idx_hbm, weights_hbm,
    out_ref,
    green, couplings, pair_atoms, shift_idx, weights, packed, held, result, landed, left_table, right_table,
    load_sem, in_send, in_recv, side_send, side_recv, out_send, out_recv,
):
    moms, energies, modes, orbitals, group = sizes
    lanes = 2 * orbitals
    rows = orbitals // 2
    cores = moms // HALVES
    here = lax.axis_index("energy")
    mom = lax.axis_index("mom")
    half, core = mom // cores, mom % cores

    def device(at, half_at, core_at):
        return (at, half_at * cores + core_at)

    def around(base, step, size):
        return lax.rem(base + step, size)

    barrier = pltpu.get_barrier_semaphore()
    for turn in range(HALVES):
        for step in range(1 if turn == 0 else 0, energies):
            pl.semaphore_signal(
                barrier, inc=1,
                device_id=device(around(here, step, energies), around(half, turn, HALVES), core),
                device_id_type=MESH,
            )
    for turn in range(1, cores):
        pl.semaphore_signal(
            barrier, inc=1, device_id=device(here, half, around(core, turn, cores)), device_id_type=MESH
        )

    load_green = pltpu.make_async_copy(green_hbm, green, load_sem.at[0])
    load_green.start()
    load_couplings = pltpu.make_async_copy(couplings_hbm, couplings, load_sem.at[1])
    load_couplings.start()
    load_small = [
        pltpu.make_async_copy(pair_atoms_hbm, pair_atoms, load_sem.at[2]),
        pltpu.make_async_copy(shift_idx_hbm, shift_idx, load_sem.at[3]),
        pltpu.make_async_copy(weights_hbm, weights, load_sem.at[4]),
    ]
    for load in load_small:
        load.start()

    edge = jnp.zeros((SHIFT_MAX, rows, lanes), jnp.float32)
    for source in range(moms):
        held[source, pl.ds(0, SHIFT_MAX)] = edge
        held[source, pl.ds(SHIFT_MAX + energies, SHIFT_MAX)] = edge

    load_green.wait()
    mask = left_lanes((rows, lanes))
    for pair in range(energies):
        top = green[0, 0, pair, pl.ds(0, rows), :]
        bottom = green[0, 0, pair, pl.ds(rows, rows), :]
        packed[0, pair] = jnp.where(mask, top, pltpu.roll(bottom, orbitals, 1))
        packed[1, pair] = jnp.where(mask, pltpu.roll(top, orbitals, 1), bottom)

    pl.semaphore_wait(barrier, HALVES * energies - 1 + cores - 1)

    reach = energies // 2
    place = lax.rem(here, reach)

    def line(far, turn):
        return lax.rem(here // reach + far, 2) * reach + lax.rem(place + turn, reach)

    def partner(slot):
        return line(slot // reach, slot % reach)

    def origin(slot):
        return line(slot // reach, (reach - slot % reach) % reach)

    def send_in(turn, slot):
        to_half, to = around(half, turn, HALVES), partner(slot)
        return pltpu.make_async_remote_copy(
            src_ref=packed.at[to_half, to],
            dst_ref=held.at[mom, SHIFT_MAX + here],
            send_sem=in_send.at[turn, slot],
            recv_sem=in_recv.at[turn, slot],
            device_id=device(to, to_half, core),
            device_id_type=MESH,
        )

    def send_side(turn, slot, side):
        source = around(half, turn, HALVES) * cores + core
        row = SHIFT_MAX + origin(slot)
        return pltpu.make_async_remote_copy(
            src_ref=held.at[source, row],
            dst_ref=held.at[source, row],
            send_sem=side_send.at[side, turn, slot],
            recv_sem=side_recv.at[side, turn, slot],
            device_id=device(here, half, around(core, side, cores)),
            device_id_type=MESH,
        )

    near_first = [(turn, slot) for slot in range(energies) for turn in range(HALVES)]
    far_first = [(turn, slot) for slot in (*range(reach, energies), *range(reach)) for turn in range(HALVES)]
    for turn, slot in far_first:
        if (turn, slot) != (0, 0):
            send_in(turn, slot).start()

    held[mom, SHIFT_MAX + here] = packed[half, here]

    load_couplings.wait()
    for load in load_small:
        load.wait()
    atom_a = pair_atoms[0, here]
    atom_b = pair_atoms[1, here]
    pick_same = (iota((orbitals, lanes), 0) == iota((orbitals, lanes), 1) % orbitals).astype(jnp.bfloat16)
    pick_other = (
        iota((orbitals, lanes), 0) == (iota((orbitals, lanes), 1) + rows) % orbitals
    ).astype(jnp.bfloat16)
    upper = iota((orbitals, lanes), 0) < rows
    same_block = (iota((lanes, lanes), 0) < orbitals) == (iota((lanes, lanes), 1) < orbitals)
    for mode in range(modes):
        left = couplings[atom_a, mode]
        right = couplings[atom_b, mode]
        left_same = jnp.dot(left, pick_same, preferred_element_type=jnp.float32)
        left_other = jnp.dot(left, pick_other, preferred_element_type=jnp.float32)
        left_table[:, pl.ds(mode * lanes, lanes)] = jnp.where(upper, left_same, left_other).astype(jnp.bfloat16)
        wide = jnp.dot(right, pick_same, preferred_element_type=jnp.float32).astype(jnp.bfloat16)
        tall = jnp.concatenate([wide, wide], axis=0)
        diagonal = jnp.where(same_block, tall.astype(jnp.float32), 0.0).astype(jnp.bfloat16)
        right_table[mode] = jnp.concatenate([diagonal, diagonal], axis=1)

    for turn, slot in near_first:
        if (turn, slot) != (0, 0):
            send_in(turn, slot).wait_recv()
        for side in range(1, cores):
            send_side(turn, slot, side).start()
    for turn, slot in near_first:
        for side in range(1, cores):
            send_side(turn, slot, side).wait_recv()

    def send_out(turn, slot):
        to_half, to = around(half, turn, HALVES), partner(slot)
        return pltpu.make_async_remote_copy(
            src_ref=result.at[to_half, to],
            dst_ref=landed.at[half, here],
            send_sem=out_send.at[turn, slot],
            recv_sem=out_recv.at[turn, slot],
            device_id=device(to, to_half, core),
            device_id_type=MESH,
        )

    def one_group(index, carry):
        first = lax.rem(reach + index * group, energies)
        sums = [[] for _ in range(modes)]
        for member in range(group):
            energy = partner(first + member)
            for mode in range(modes):
                shift = shift_idx[mode]
                totals = [None] * HALVES
                for offset in range(moms):
                    source = lax.rem(core - offset + moms, moms)
                    for sign, slot in ((0, energy - shift), (1, energy + shift)):
                        value = held[source, SHIFT_MAX + slot]
                        for target in range(HALVES):
                            term = weights[mode, sign, (target * cores + offset) % moms] * value
                            totals[target] = term if totals[target] is None else totals[target] + term
                sums[mode].extend(totals)
        rights = []
        for mode in range(modes):
            high, low = split(jnp.concatenate(sums[mode], axis=0))
            rights.append(
                lax.dot_general(
                    jnp.concatenate([high, low], axis=1), right_table[mode],
                    (((1,), (1,)), ((), ())), preferred_element_type=jnp.float32,
                )
            )
        for member in range(group):
            columns = []
            for target in range(HALVES):
                start = (member * HALVES + target) * rows
                stack = []
                for mode in range(modes):
                    block = rights[mode][start:start + rows]
                    high, low = split(jnp.concatenate([block, pltpu.roll(block, orbitals, 1)], axis=0))
                    stack += [high, low]
                columns.append(jnp.concatenate(stack, axis=0))
            product = jnp.dot(
                left_table[...], jnp.concatenate(columns, axis=1), preferred_element_type=jnp.float32
            )
            energy = partner(first + member)
            for target in range(HALVES):
                both = product[:, target * lanes:(target + 1) * lanes]
                result[target, energy] = jnp.where(mask, both[:rows], both[rows:])
                own = jnp.logical_and(energy == here, half == target)
                turn = lax.rem(target - half + HALVES, HALVES)

                @pl.when(jnp.logical_not(own))
                def _():
                    send_out(turn, first + member).start()

        return carry

    lax.fori_loop(0, energies // group, one_group, 0)
    landed[half, here] = result[half, here]

    for slot in (*range(reach, energies), *range(reach)):
        for turn in range(HALVES):
            if (turn, slot) != (0, 0):
                send_out(turn, slot).wait_recv()
        pair = origin(slot)
        real, imag = landed[0, pair], landed[1, pair]
        out_ref[0, 0, pair, pl.ds(0, rows), :] = jnp.where(mask, real, pltpu.roll(imag, orbitals, 1))
        out_ref[0, 0, pair, pl.ds(rows, rows), :] = jnp.where(mask, pltpu.roll(real, orbitals, 1), imag)

    for turn, slot in near_first:
        if (turn, slot) != (0, 0):
            send_in(turn, slot).wait_send()
            send_out(turn, slot).wait_send()
        for side in range(1, cores):
            send_side(turn, slot, side).wait_send()


def on_device(moms, energies, green_less, couplings, pair_atoms, shift_idx, weights):
    modes, orbitals = couplings.shape[1], couplings.shape[2]
    lanes, rows, cores = 2 * orbitals, orbitals // 2, moms // HALVES
    group = next(size for size in (2, 1) if energies // 2 % size == 0)
    atoms_first = pair_atoms.T
    modes_first = weights.transpose(1, 0, 2)
    hbm = pl.BlockSpec(memory_space=pl.ANY)
    dma = pltpu.SemaphoreType.DMA
    return pl.pallas_call(
        functools.partial(kernel, (moms, energies, modes, orbitals, group)),
        out_shape=jax.ShapeDtypeStruct(green_less.shape, jnp.float32),
        in_specs=[hbm] * 5,
        out_specs=pl.BlockSpec(memory_space=pltpu.VMEM),
        scratch_shapes=[
            pltpu.VMEM(green_less.shape, jnp.float32),
            pltpu.VMEM(couplings.shape, jnp.bfloat16),
            pltpu.SMEM(atoms_first.shape, jnp.int32),
            pltpu.SMEM(shift_idx.shape, jnp.int32),
            pltpu.SMEM(modes_first.shape, jnp.float32),
            pltpu.VMEM((HALVES, energies, rows, lanes), jnp.float32),
            pltpu.VMEM((moms, energies + 2 * SHIFT_MAX, rows, lanes), jnp.float32),
            pltpu.VMEM((HALVES, energies, rows, lanes), jnp.float32),
            pltpu.VMEM((HALVES, energies, rows, lanes), jnp.float32),
            pltpu.VMEM((orbitals, modes * lanes), jnp.bfloat16),
            pltpu.VMEM((modes, lanes, 2 * lanes), jnp.bfloat16),
            dma((5,)),
            dma((HALVES, energies)),
            dma((HALVES, energies)),
            dma((cores, HALVES, energies)),
            dma((cores, HALVES, energies)),
            dma((HALVES, energies)),
            dma((HALVES, energies)),
        ],
        compiler_params=pltpu.CompilerParams(
            collective_id=0, has_side_effects=True, vmem_limit_bytes=60 * 2**20
        ),
    )(green_less, couplings, atoms_first, shift_idx, modes_first)


def solution(mesh):
    spec = P("mom", "energy", None, None, None)
    return jax.shard_map(
        functools.partial(on_device, mesh.shape["mom"], mesh.shape["energy"]),
        mesh=mesh,
        in_specs=(spec, P(), P(), P(), P()),
        out_specs=spec,
        check_vma=False,
    )
```

```python
import functools

import jax
import jax.numpy as jnp
from jax import lax
from jax.experimental import pallas as pl
from jax.experimental.pallas import tpu as pltpu
from jax.sharding import PartitionSpec as P

HALVES = 2
ROWS = 2
SHIFT_MAX = 4
MESH = pl.DeviceIdType.MESH


def split(value):
    high = value.astype(jnp.bfloat16)
    return high, (value - high.astype(jnp.float32)).astype(jnp.bfloat16)


def left_lanes(shape):
    return lax.broadcasted_iota(jnp.int32, shape, len(shape) - 1) < shape[-1] // 2


def iota(shape, axis):
    return lax.broadcasted_iota(jnp.int32, shape, axis)


def kernel(
    sizes,
    green_hbm, couplings_hbm, pair_atoms_hbm, shift_idx_hbm, weights_hbm,
    out_hbm,
    green, couplings, pair_atoms, shift_idx, weights, packed, held_real, held_imag, result, landed, out,
    left_table, right_table,
    load_sem, store_sem, in_send, in_recv, up_send, up_recv, side_send, side_recv,
    relay_send, relay_recv, out_send, out_recv,
):
    moms, energies, modes, orbitals, group = sizes
    lanes = 2 * orbitals
    rows = orbitals // 2
    cores = moms // ROWS
    held = (held_real, held_imag)
    here = lax.axis_index("energy")
    mom = lax.axis_index("mom")
    line, core = mom // cores, mom % cores

    def around(base, step, size):
        return lax.rem(base + step, size)

    def along(step):
        return (around(here, step, energies), mom)

    def above(turn):
        return (here, around(line, turn, ROWS) * cores + core)

    def beside(turn):
        return (here, line * cores + around(core, turn, cores))

    barrier = pltpu.get_barrier_semaphore()
    partners = [along(step) for step in range(1, energies)]
    partners += [above(turn) for turn in range(1, ROWS)]
    partners += [beside(turn) for turn in range(1, cores)]
    for partner in partners:
        pl.semaphore_signal(barrier, inc=1, device_id=partner, device_id_type=MESH)

    load_green = pltpu.make_async_copy(green_hbm, green, load_sem.at[0])
    load_green.start()
    load_couplings = pltpu.make_async_copy(couplings_hbm, couplings, load_sem.at[1])
    load_couplings.start()
    load_small = [
        pltpu.make_async_copy(pair_atoms_hbm, pair_atoms, load_sem.at[2]),
        pltpu.make_async_copy(shift_idx_hbm, shift_idx, load_sem.at[3]),
        pltpu.make_async_copy(weights_hbm, weights, load_sem.at[4]),
    ]
    for load in load_small:
        load.start()

    edge = jnp.zeros((SHIFT_MAX, rows, lanes), jnp.float32)
    for half in range(HALVES):
        for source in range(moms):
            held[half][source, pl.ds(0, SHIFT_MAX)] = edge
            held[half][source, pl.ds(SHIFT_MAX + energies, SHIFT_MAX)] = edge

    load_green.wait()
    mask = left_lanes((rows, lanes))
    for pair in range(energies):
        top = green[0, 0, pair, pl.ds(0, rows), :]
        bottom = green[0, 0, pair, pl.ds(rows, rows), :]
        packed[0, pair] = jnp.where(mask, top, pltpu.roll(bottom, orbitals, 1))
        packed[1, pair] = jnp.where(mask, pltpu.roll(top, orbitals, 1), bottom)

    pl.semaphore_wait(barrier, len(partners))

    def remote(source, target, send_sem, recv_sem, device):
        return pltpu.make_async_remote_copy(
            src_ref=source, dst_ref=target, send_sem=send_sem, recv_sem=recv_sem,
            device_id=device, device_id_type=MESH,
        )

    def row(step):
        return SHIFT_MAX + around(here, energies - step, energies)

    def send_in(half, step):
        return remote(
            packed.at[half, around(here, step, energies)], held[half].at[mom, SHIFT_MAX + here],
            in_send.at[half, step], in_recv.at[half, step], along(step),
        )

    def send_up(half, step, turn):
        block = held[half].at[mom, row(step)]
        return remote(block, block, up_send.at[turn, half, step], up_recv.at[turn, half, step], above(turn))

    def send_side(half, step, turn):
        block = held[half].at[mom, row(step)]
        return remote(block, block, side_send.at[turn, half, step], side_recv.at[turn, half, step], beside(turn))

    def send_relay(half, step, up, turn):
        source = around(line, ROWS - up, ROWS) * cores + core
        block = held[half].at[source, row(step)]
        index = (up * cores + turn, half, step)
        return remote(block, block, relay_send.at[index], relay_recv.at[index], beside(turn))

    def send_out(half, step):
        return remote(
            result.at[half, around(here, step, energies)], landed.at[half, here],
            out_send.at[half, step], out_recv.at[half, step], along(step),
        )

    far_first = sorted(range(energies), key=lambda step: -min(step, energies - step))
    near_first = far_first[::-1]
    for half in range(HALVES):
        for step in far_first[:-1]:
            send_in(half, step).start()
    for half in range(HALVES):
        held[half][mom, SHIFT_MAX + here] = packed[half, here]

    load_couplings.wait()
    for load in load_small:
        load.wait()
    atom_a = pair_atoms[0, here]
    atom_b = pair_atoms[1, here]
    pick_same = (iota((orbitals, lanes), 0) == iota((orbitals, lanes), 1) % orbitals).astype(jnp.bfloat16)
    pick_other = (
        iota((orbitals, lanes), 0) == (iota((orbitals, lanes), 1) + rows) % orbitals
    ).astype(jnp.bfloat16)
    upper = iota((orbitals, lanes), 0) < rows
    same_block = (iota((lanes, lanes), 0) < orbitals) == (iota((lanes, lanes), 1) < orbitals)
    for mode in range(modes):
        left = couplings[atom_a, mode]
        right = couplings[atom_b, mode]
        left_same = jnp.dot(left, pick_same, preferred_element_type=jnp.float32)
        left_other = jnp.dot(left, pick_other, preferred_element_type=jnp.float32)
        left_table[:, pl.ds(mode * lanes, lanes)] = jnp.where(upper, left_same, left_other).astype(jnp.bfloat16)
        wide = jnp.dot(right, pick_same, preferred_element_type=jnp.float32).astype(jnp.bfloat16)
        tall = jnp.concatenate([wide, wide], axis=0)
        diagonal = jnp.where(same_block, tall.astype(jnp.float32), 0.0).astype(jnp.bfloat16)
        right_table[mode] = jnp.concatenate([diagonal, diagonal], axis=1)

    def spread(half, steps):
        for step in steps:
            if step:
                send_in(half, step).wait_recv()
            for turn in range(1, ROWS):
                send_up(half, step, turn).start()
            for turn in range(1, cores):
                send_side(half, step, turn).start()

    def pass_on(half):
        for step in near_first:
            for up in range(1, ROWS):
                send_up(half, step, up).wait_recv()
                for turn in range(1, cores):
                    send_relay(half, step, up, turn).start()

    def gather(half):
        for step in near_first:
            for turn in range(1, cores):
                send_side(half, step, turn).wait_recv()
                for up in range(1, ROWS):
                    send_relay(half, step, up, turn).wait_recv()

    def compute(half):
        def one_group(index, carry):
            steps = []
            for member in range(group):
                reach = index * (group // 2) + (member + 1) // 2
                steps.append(energies // 2 + (reach if member % 2 == 0 else -reach))
            sums = [[] for _ in range(modes)]
            for step in steps:
                energy = around(here, step, energies)
                for mode in range(modes):
                    shift = shift_idx[mode]
                    total = None
                    for offset in range(moms):
                        source = lax.rem(mom - offset + moms, moms)
                        for sign, at in ((0, energy - shift), (1, energy + shift)):
                            term = weights[mode, sign, offset] * held[half][source, SHIFT_MAX + at]
                            total = term if total is None else total + term
                    sums[mode].append(total)
            rights = []
            for mode in range(modes):
                high, low = split(jnp.concatenate(sums[mode], axis=0))
                rights.append(
                    lax.dot_general(
                        jnp.concatenate([high, low], axis=1), right_table[mode],
                        (((1,), (1,)), ((), ())), preferred_element_type=jnp.float32,
                    )
                )
            columns = []
            for member in range(group):
                stack = []
                for mode in range(modes):
                    block = rights[mode][member * rows:(member + 1) * rows]
                    high, low = split(jnp.concatenate([block, pltpu.roll(block, orbitals, 1)], axis=0))
                    stack += [high, low]
                columns.append(jnp.concatenate(stack, axis=0))
            product = jnp.dot(
                left_table[...], jnp.concatenate(columns, axis=1), preferred_element_type=jnp.float32
            )
            for member, step in enumerate(steps):
                both = product[:, member * lanes:(member + 1) * lanes]
                result[half, around(here, step, energies)] = jnp.where(mask, both[:rows], both[rows:])

                @pl.when(step > 0)
                def _():
                    send_out(half, step).start()

            return carry

        lax.fori_loop(0, energies // group, one_group, 0)
        landed[half, here] = result[half, here]

    early, late = near_first[:energies // 2], near_first[energies // 2:]
    spread(0, near_first)
    pass_on(0)
    spread(1, early)
    gather(0)
    compute(0)
    spread(1, late)
    pass_on(1)
    gather(1)
    compute(1)

    def store(pair):
        return pltpu.make_async_copy(out.at[0, 0, pair], out_hbm.at[0, 0, pair], store_sem.at[pair])

    for step in (0, *far_first[:-1]):
        if step:
            for half in range(HALVES):
                send_out(half, step).wait_recv()
        pair = around(here, energies - step, energies)
        real, imag = landed[0, pair], landed[1, pair]
        out[0, 0, pair, pl.ds(0, rows), :] = jnp.where(mask, real, pltpu.roll(imag, orbitals, 1))
        out[0, 0, pair, pl.ds(rows, rows), :] = jnp.where(mask, pltpu.roll(real, orbitals, 1), imag)
        store(pair).start()

    for half in range(HALVES):
        for step in near_first:
            if step:
                send_in(half, step).wait_send()
                send_out(half, step).wait_send()
            for turn in range(1, cores):
                send_side(half, step, turn).wait_send()
            for up in range(1, ROWS):
                send_up(half, step, up).wait_send()
                for turn in range(1, cores):
                    send_relay(half, step, up, turn).wait_send()
    for pair in range(energies):
        store(pair).wait()


def on_device(moms, energies, green_less, couplings, pair_atoms, shift_idx, weights):
    modes, orbitals = couplings.shape[1], couplings.shape[2]
    lanes, rows, cores = 2 * orbitals, orbitals // 2, moms // ROWS
    group = next(size for size in (4, 2) if energies % size == 0)
    atoms_first = pair_atoms.T
    modes_first = weights.transpose(1, 0, 2)
    hbm = pl.BlockSpec(memory_space=pl.ANY)
    dma = pltpu.SemaphoreType.DMA
    return pl.pallas_call(
        functools.partial(kernel, (moms, energies, modes, orbitals, group)),
        out_shape=jax.ShapeDtypeStruct(green_less.shape, jnp.float32),
        in_specs=[hbm] * 5,
        out_specs=hbm,
        scratch_shapes=[
            pltpu.VMEM(green_less.shape, jnp.float32),
            pltpu.VMEM(couplings.shape, jnp.bfloat16),
            pltpu.SMEM(atoms_first.shape, jnp.int32),
            pltpu.SMEM(shift_idx.shape, jnp.int32),
            pltpu.SMEM(modes_first.shape, jnp.float32),
            pltpu.VMEM((HALVES, energies, rows, lanes), jnp.float32),
            pltpu.VMEM((moms, energies + 2 * SHIFT_MAX, rows, lanes), jnp.float32),
            pltpu.VMEM((moms, energies + 2 * SHIFT_MAX, rows, lanes), jnp.float32),
            pltpu.VMEM((HALVES, energies, rows, lanes), jnp.float32),
            pltpu.VMEM((HALVES, energies, rows, lanes), jnp.float32),
            pltpu.VMEM(green_less.shape, jnp.float32),
            pltpu.VMEM((orbitals, modes * lanes), jnp.bfloat16),
            pltpu.VMEM((modes, lanes, 2 * lanes), jnp.bfloat16),
            dma((5,)),
            dma((energies,)),
            dma((HALVES, energies)),
            dma((HALVES, energies)),
            dma((ROWS, HALVES, energies)),
            dma((ROWS, HALVES, energies)),
            dma((cores, HALVES, energies)),
            dma((cores, HALVES, energies)),
            dma((ROWS * cores, HALVES, energies)),
            dma((ROWS * cores, HALVES, energies)),
            dma((HALVES, energies)),
            dma((HALVES, energies)),
        ],
        compiler_params=pltpu.CompilerParams(
            collective_id=0, has_side_effects=True, vmem_limit_bytes=60 * 2**20
        ),
    )(green_less, couplings, atoms_first, shift_idx, modes_first)


def solution(mesh):
    spec = P("mom", "energy", None, None, None)
    return jax.shard_map(
        functools.partial(on_device, mesh.shape["mom"], mesh.shape["energy"]),
        mesh=mesh,
        in_specs=(spec, P(), P(), P(), P()),
        out_specs=spec,
        check_vma=False,
    )
```

```python
import functools

import jax
import jax.numpy as jnp
from jax import lax
from jax.experimental import pallas as pl
from jax.experimental.pallas import tpu as pltpu
from jax.sharding import PartitionSpec as P

HALVES = 2
SHIFT_MAX = 4
MESH = pl.DeviceIdType.MESH


def split(value):
    high = value.astype(jnp.bfloat16)
    return high, (value - high.astype(jnp.float32)).astype(jnp.bfloat16)


def left_lanes(shape):
    return lax.broadcasted_iota(jnp.int32, shape, len(shape) - 1) < shape[-1] // 2


def iota(shape, axis):
    return lax.broadcasted_iota(jnp.int32, shape, axis)


def kernel(
    sizes,
    green_hbm, couplings_hbm, pair_atoms_hbm, shift_idx_hbm, weights_hbm,
    out_hbm,
    green, couplings, pair_atoms, shift_idx, weights, packed, held, result, landed, out, left_table, right_table,
    load_sem, store_sem, in_send, in_recv, side_send, side_recv, out_send, out_recv,
):
    moms, energies, modes, orbitals, group = sizes
    reach = energies // 2
    lanes = 2 * orbitals
    rows = orbitals // 2
    cores = moms // HALVES
    here = lax.axis_index("energy")
    mom = lax.axis_index("mom")
    half, core = mom // cores, mom % cores

    def device(at, half_at, core_at):
        return (at, half_at * cores + core_at)

    def around(base, step, size):
        return lax.rem(base + step, size)

    barrier = pltpu.get_barrier_semaphore()
    for turn in range(HALVES):
        for step in range(1 if turn == 0 else 0, energies):
            pl.semaphore_signal(
                barrier, inc=1,
                device_id=device(around(here, step, energies), around(half, turn, HALVES), core),
                device_id_type=MESH,
            )
    for turn in range(1, cores):
        pl.semaphore_signal(
            barrier, inc=1, device_id=device(here, half, around(core, turn, cores)), device_id_type=MESH
        )

    load_green = pltpu.make_async_copy(green_hbm, green, load_sem.at[0])
    load_green.start()
    load_couplings = pltpu.make_async_copy(couplings_hbm, couplings, load_sem.at[1])
    load_couplings.start()
    load_small = [
        pltpu.make_async_copy(pair_atoms_hbm, pair_atoms, load_sem.at[2]),
        pltpu.make_async_copy(shift_idx_hbm, shift_idx, load_sem.at[3]),
        pltpu.make_async_copy(weights_hbm, weights, load_sem.at[4]),
    ]
    for load in load_small:
        load.start()

    edge = jnp.zeros((SHIFT_MAX, rows, lanes), jnp.float32)
    for source in range(moms):
        held[source, pl.ds(0, SHIFT_MAX)] = edge
        held[source, pl.ds(SHIFT_MAX + energies, SHIFT_MAX)] = edge

    load_green.wait()
    mask = left_lanes((rows, lanes))
    for pair in range(energies):
        top = green[0, 0, pair, pl.ds(0, rows), :]
        bottom = green[0, 0, pair, pl.ds(rows, rows), :]
        packed[0, pair] = jnp.where(mask, top, pltpu.roll(bottom, orbitals, 1))
        packed[1, pair] = jnp.where(mask, pltpu.roll(top, orbitals, 1), bottom)

    pl.semaphore_wait(barrier, HALVES * energies - 1 + cores - 1)

    def send_in(turn, step):
        to_half, to = around(half, turn, HALVES), around(here, step, energies)
        return pltpu.make_async_remote_copy(
            src_ref=packed.at[to_half, to],
            dst_ref=held.at[mom, SHIFT_MAX + here],
            send_sem=in_send.at[turn, step],
            recv_sem=in_recv.at[turn, here],
            device_id=device(to, to_half, core),
            device_id_type=MESH,
        )

    def send_side(turn, far, side):
        source = around(half, turn, HALVES) * cores + core
        base = around(here // reach, far, energies // reach) * reach
        block = held.at[source, pl.ds(SHIFT_MAX + base, reach)]
        return pltpu.make_async_remote_copy(
            src_ref=block,
            dst_ref=block,
            send_sem=side_send.at[side, turn, far],
            recv_sem=side_recv.at[side, turn, far],
            device_id=device(here, half, around(core, side, cores)),
            device_id_type=MESH,
        )

    def arrive_in(turn, source):
        def wait():
            slot = held.at[around(half, turn, HALVES) * cores + core, SHIFT_MAX + source]
            pltpu.make_async_remote_copy(
                src_ref=slot, dst_ref=slot, send_sem=in_send.at[turn, 0], recv_sem=in_recv.at[turn, source],
                device_id=device(here, half, around(core, 1, cores)), device_id_type=MESH,
            ).wait_recv()

        if turn == 0:
            pl.when(source != here)(wait)
        else:
            wait()

    far_first = sorted(range(energies), key=lambda step: -min(step, energies - step))
    slots = [(turn, step) for step in far_first for turn in range(HALVES)]
    near_first = slots[::-1]
    remote = [slot for slot in slots if slot != (0, 0)]
    for turn, step in remote:
        send_in(turn, step).start()

    held[mom, SHIFT_MAX + here] = packed[half, here]

    load_couplings.wait()
    for load in load_small:
        load.wait()
    atom_a = pair_atoms[0, here]
    atom_b = pair_atoms[1, here]
    pick_same = (iota((orbitals, lanes), 0) == iota((orbitals, lanes), 1) % orbitals).astype(jnp.bfloat16)
    pick_other = (
        iota((orbitals, lanes), 0) == (iota((orbitals, lanes), 1) + rows) % orbitals
    ).astype(jnp.bfloat16)
    upper = iota((orbitals, lanes), 0) < rows
    same_block = (iota((lanes, lanes), 0) < orbitals) == (iota((lanes, lanes), 1) < orbitals)
    for mode in range(modes):
        left = couplings[atom_a, mode]
        right = couplings[atom_b, mode]
        left_same = jnp.dot(left, pick_same, preferred_element_type=jnp.float32)
        left_other = jnp.dot(left, pick_other, preferred_element_type=jnp.float32)
        left_table[:, pl.ds(mode * lanes, lanes)] = jnp.where(upper, left_same, left_other).astype(jnp.bfloat16)
        wide = lax.dot_general(
            right, pick_same, (((0,), (0,)), ((), ())), preferred_element_type=jnp.float32
        ).astype(jnp.bfloat16)
        tall = jnp.concatenate([wide, wide], axis=0)
        diagonal = jnp.where(same_block, tall.astype(jnp.float32), 0.0).astype(jnp.bfloat16)
        right_table[mode] = jnp.concatenate([diagonal, diagonal], axis=0)

    chunks = [(turn, far) for far in range(energies // reach) for turn in range(HALVES)]
    for turn, far in chunks:
        base = around(here // reach, far, energies // reach) * reach
        for member in range(reach):
            arrive_in(turn, base + member)
        for side in range(1, cores):
            send_side(turn, far, side).start()
    for turn, far in chunks:
        for side in range(1, cores):
            send_side(turn, far, side).wait_recv()

    def send_out(to_half, to):
        turn = lax.rem(to_half - half + HALVES, HALVES)
        step = lax.rem(to - here + energies, energies)
        return pltpu.make_async_remote_copy(
            src_ref=result.at[to_half, to],
            dst_ref=landed.at[half, here],
            send_sem=out_send.at[turn, step],
            recv_sem=out_recv.at[turn, step],
            device_id=device(to, to_half, core),
            device_id_type=MESH,
        )

    def one_group(index, carry):
        first = lax.rem(here // group + 1 + index, energies // group) * group
        sums = [[] for _ in range(modes)]
        for member in range(group):
            energy = first + member
            for mode in range(modes):
                shift = shift_idx[mode]
                totals = [None] * HALVES
                for offset in range(moms):
                    source = lax.rem(core - offset + moms, moms)
                    for sign, slot in ((0, energy - shift), (1, energy + shift)):
                        value = held[source, SHIFT_MAX + slot]
                        for target in range(HALVES):
                            term = weights[mode, sign, (target * cores + offset) % moms] * value
                            totals[target] = term if totals[target] is None else totals[target] + term
                sums[mode].extend(totals)
        rights = []
        for mode in range(modes):
            high, low = split(jnp.concatenate(sums[mode], axis=0))
            rights.append(
                jnp.dot(
                    jnp.concatenate([high, low], axis=1), right_table[mode],
                    preferred_element_type=jnp.float32,
                )
            )
        for member in range(group):
            columns = []
            for target in range(HALVES):
                start = (member * HALVES + target) * rows
                stack = []
                for mode in range(modes):
                    block = rights[mode][start:start + rows]
                    high, low = split(jnp.concatenate([block, pltpu.roll(block, orbitals, 1)], axis=0))
                    stack += [high, low]
                columns.append(jnp.concatenate(stack, axis=0))
            product = jnp.dot(
                left_table[...], jnp.concatenate(columns, axis=1), preferred_element_type=jnp.float32
            )
            energy = first + member
            for target in range(HALVES):
                both = product[:, target * lanes:(target + 1) * lanes]
                result[target, energy] = jnp.where(mask, both[:rows], both[rows:])
                own = jnp.logical_and(energy == here, half == target)

                @pl.when(jnp.logical_not(own))
                def _():
                    send_out(target, energy).start()

        return carry

    lax.fori_loop(0, energies // group, one_group, 0)
    landed[half, here] = result[half, here]

    def store(pair):
        return pltpu.make_async_copy(out.at[0, 0, pair], out_hbm.at[0, 0, pair], store_sem.at[pair])

    for step in reversed(far_first):
        for turn in range(HALVES):
            if (turn, step) != (0, 0):
                send_out(around(half, turn, HALVES), around(here, step, energies)).wait_recv()
        pair = around(here, energies - step, energies)
        real, imag = landed[0, pair], landed[1, pair]
        out[0, 0, pair, pl.ds(0, rows), :] = jnp.where(mask, real, pltpu.roll(imag, orbitals, 1))
        out[0, 0, pair, pl.ds(rows, rows), :] = jnp.where(mask, pltpu.roll(real, orbitals, 1), imag)
        store(pair).start()

    for turn, step in slots:
        if (turn, step) != (0, 0):
            send_in(turn, step).wait_send()
            send_out(around(half, turn, HALVES), around(here, step, energies)).wait_send()
    for turn, far in chunks:
        for side in range(1, cores):
            send_side(turn, far, side).wait_send()
    for pair in range(energies):
        store(pair).wait()


def on_device(moms, energies, green_less, couplings, pair_atoms, shift_idx, weights):
    modes, orbitals = couplings.shape[1], couplings.shape[2]
    lanes, rows, cores = 2 * orbitals, orbitals // 2, moms // HALVES
    group = next(size for size in (4, 2, 1) if energies % size == 0)
    atoms_first = pair_atoms.T
    modes_first = weights.transpose(1, 0, 2)
    hbm = pl.BlockSpec(memory_space=pl.ANY)
    dma = pltpu.SemaphoreType.DMA
    return pl.pallas_call(
        functools.partial(kernel, (moms, energies, modes, orbitals, group)),
        out_shape=jax.ShapeDtypeStruct(green_less.shape, jnp.float32),
        in_specs=[hbm] * 5,
        out_specs=hbm,
        scratch_shapes=[
            pltpu.VMEM(green_less.shape, jnp.float32),
            pltpu.VMEM(couplings.shape, jnp.bfloat16),
            pltpu.SMEM(atoms_first.shape, jnp.int32),
            pltpu.SMEM(shift_idx.shape, jnp.int32),
            pltpu.SMEM(modes_first.shape, jnp.float32),
            pltpu.VMEM((HALVES, energies, rows, lanes), jnp.float32),
            pltpu.VMEM((moms, energies + 2 * SHIFT_MAX, rows, lanes), jnp.float32),
            pltpu.VMEM((HALVES, energies, rows, lanes), jnp.float32),
            pltpu.VMEM((HALVES, energies, rows, lanes), jnp.float32),
            pltpu.VMEM(green_less.shape, jnp.float32),
            pltpu.VMEM((orbitals, modes * lanes), jnp.bfloat16),
            pltpu.VMEM((modes, 2 * lanes, lanes), jnp.bfloat16),
            dma((5,)),
            dma((energies,)),
            dma((HALVES, energies)),
            dma((HALVES, energies)),
            dma((cores, HALVES, 2)),
            dma((cores, HALVES, 2)),
            dma((HALVES, energies)),
            dma((HALVES, energies)),
        ],
        compiler_params=pltpu.CompilerParams(
            collective_id=0, has_side_effects=True, vmem_limit_bytes=60 * 2**20
        ),
    )(green_less, couplings, atoms_first, shift_idx, modes_first)


def solution(mesh):
    spec = P("mom", "energy", None, None, None)
    return jax.shard_map(
        functools.partial(on_device, mesh.shape["mom"], mesh.shape["energy"]),
        mesh=mesh,
        in_specs=(spec, P(), P(), P(), P()),
        out_specs=spec,
        check_vma=False,
    )
```

```python
import functools

import jax
import jax.numpy as jnp
from jax import lax
from jax.experimental import pallas as pl
from jax.experimental.pallas import tpu as pltpu
from jax.sharding import PartitionSpec as P

HALVES = 2
SHIFT_MAX = 4
MESH = pl.DeviceIdType.MESH


def split(value):
    high = value.astype(jnp.bfloat16)
    return high, (value - high.astype(jnp.float32)).astype(jnp.bfloat16)


def left_lanes(shape):
    return lax.broadcasted_iota(jnp.int32, shape, len(shape) - 1) < shape[-1] // 2


def iota(shape, axis):
    return lax.broadcasted_iota(jnp.int32, shape, axis)


def kernel(
    sizes,
    green_hbm, couplings_hbm, pair_atoms_hbm, shift_idx_hbm, weights_hbm,
    out,
    green, couplings, pair_atoms, shift_idx, weights, packed, held, aside, partial, result, landed, left_table, right_table,
    load_sem, in_send, in_recv, side_send, side_recv, out_send, out_recv,
):
    moms, energies, modes, orbitals, group = sizes
    reach = energies // 2
    lanes = 2 * orbitals
    rows = orbitals // 2
    cores = moms // HALVES
    here = lax.axis_index("energy")
    mom = lax.axis_index("mom")
    half, core = mom // cores, mom % cores

    def device(at, half_at, core_at):
        return (at, half_at * cores + core_at)

    def around(base, step, size):
        return lax.rem(base + step, size)

    barrier = pltpu.get_barrier_semaphore()
    for turn in range(HALVES):
        for step in range(1 if turn == 0 else 0, energies):
            pl.semaphore_signal(
                barrier, inc=1,
                device_id=device(around(here, step, energies), around(half, turn, HALVES), core),
                device_id_type=MESH,
            )
    for turn in range(1, cores):
        pl.semaphore_signal(
            barrier, inc=1, device_id=device(here, half, around(core, turn, cores)), device_id_type=MESH
        )

    load_green = pltpu.make_async_copy(green_hbm, green, load_sem.at[0])
    load_green.start()
    load_couplings = pltpu.make_async_copy(couplings_hbm, couplings, load_sem.at[1])
    load_couplings.start()
    load_small = [
        pltpu.make_async_copy(pair_atoms_hbm, pair_atoms, load_sem.at[2]),
        pltpu.make_async_copy(shift_idx_hbm, shift_idx, load_sem.at[3]),
        pltpu.make_async_copy(weights_hbm, weights, load_sem.at[4]),
    ]
    for load in load_small:
        load.start()

    edge = jnp.zeros((SHIFT_MAX, rows, lanes), jnp.float32)
    for source in range(HALVES):
        held[source, pl.ds(0, SHIFT_MAX)] = edge
        held[source, pl.ds(SHIFT_MAX + energies, SHIFT_MAX)] = edge
        for side in range(1, cores):
            aside[side - 1, source, pl.ds(0, SHIFT_MAX)] = edge
            aside[side - 1, source, pl.ds(SHIFT_MAX + energies, SHIFT_MAX)] = edge

    load_green.wait()
    mask = left_lanes((rows, lanes))
    for pair in range(energies):
        top = green[0, 0, pair, pl.ds(0, rows), :]
        bottom = green[0, 0, pair, pl.ds(rows, rows), :]
        packed[0, pair] = jnp.where(mask, top, pltpu.roll(bottom, orbitals, 1))
        packed[1, pair] = jnp.where(mask, pltpu.roll(top, orbitals, 1), bottom)

    pl.semaphore_wait(barrier, HALVES * energies - 1 + cores - 1)

    def send_in(turn, step):
        to_half, to = around(half, turn, HALVES), around(here, step, energies)
        return pltpu.make_async_remote_copy(
            src_ref=packed.at[to_half, to],
            dst_ref=held.at[half, SHIFT_MAX + here],
            send_sem=in_send.at[turn, step],
            recv_sem=in_recv.at[turn, here],
            device_id=device(to, to_half, core),
            device_id_type=MESH,
        )

    def send_side(turn, far, side):
        source = around(half, turn, HALVES)
        base = around(here // reach, far, energies // reach) * reach
        block = pl.ds(SHIFT_MAX + base, reach)
        return pltpu.make_async_remote_copy(
            src_ref=held.at[source, block],
            dst_ref=aside.at[side - 1, source, block],
            send_sem=side_send.at[side, turn, far],
            recv_sem=side_recv.at[side, turn, far],
            device_id=device(here, half, around(core, side, cores)),
            device_id_type=MESH,
        )

    def arrive_in(turn, source):
        def wait():
            slot = held.at[around(half, turn, HALVES), SHIFT_MAX + source]
            pltpu.make_async_remote_copy(
                src_ref=slot, dst_ref=slot, send_sem=in_send.at[turn, 0], recv_sem=in_recv.at[turn, source],
                device_id=device(here, half, around(core, 1, cores)), device_id_type=MESH,
            ).wait_recv()

        if turn == 0:
            pl.when(source != here)(wait)
        else:
            wait()

    far_first = sorted(range(energies), key=lambda step: -min(step, energies - step))
    slots = [(turn, step) for step in far_first for turn in range(HALVES)]
    near_first = slots[::-1]
    remote = [slot for slot in slots if slot != (0, 0)]
    for turn, step in remote:
        send_in(turn, step).start()

    held[half, SHIFT_MAX + here] = packed[half, here]

    load_couplings.wait()
    for load in load_small:
        load.wait()
    atom_a = pair_atoms[0, here]
    atom_b = pair_atoms[1, here]
    pick_same = (iota((orbitals, lanes), 0) == iota((orbitals, lanes), 1) % orbitals).astype(jnp.bfloat16)
    pick_other = (
        iota((orbitals, lanes), 0) == (iota((orbitals, lanes), 1) + rows) % orbitals
    ).astype(jnp.bfloat16)
    upper = iota((orbitals, lanes), 0) < rows
    same_block = (iota((lanes, lanes), 0) < orbitals) == (iota((lanes, lanes), 1) < orbitals)
    for mode in range(modes):
        left = couplings[atom_a, mode]
        right = couplings[atom_b, mode]
        left_same = jnp.dot(left, pick_same, preferred_element_type=jnp.float32)
        left_other = jnp.dot(left, pick_other, preferred_element_type=jnp.float32)
        left_table[:, pl.ds(mode * lanes, lanes)] = jnp.where(upper, left_same, left_other).astype(jnp.bfloat16)
        wide = lax.dot_general(
            right, pick_same, (((0,), (0,)), ((), ())), preferred_element_type=jnp.float32
        ).astype(jnp.bfloat16)
        tall = jnp.concatenate([wide, wide], axis=0)
        diagonal = jnp.where(same_block, tall.astype(jnp.float32), 0.0).astype(jnp.bfloat16)
        right_table[mode] = jnp.concatenate([diagonal, diagonal], axis=0)

    chunks = [(turn, far) for far in range(energies // reach) for turn in range(HALVES)]
    for turn, far in chunks:
        base = around(here // reach, far, energies // reach) * reach
        for member in range(reach):
            arrive_in(turn, base + member)
        for side in range(1, cores):
            send_side(turn, far, side).start()
    def mix(block, energy, mode, offset, totals):
        shift = shift_idx[mode]
        for row in range(HALVES):
            source = lax.rem(row + HALVES - (offset > core).astype(jnp.int32), HALVES)
            for sign, slot in ((0, energy - shift), (1, energy + shift)):
                value = block[source, SHIFT_MAX + slot]
                for target in range(HALVES):
                    turn = ((target - row) * cores + offset) % moms
                    term = weights[mode, sign, turn] * value
                    totals[target] = term if totals[target] is None else totals[target] + term
        return totals

    def own_part(index, carry):
        for member in range(group):
            energy = index * group + member
            for mode in range(modes):
                totals = mix(held, energy, mode, 0, [None] * HALVES)
                for target in range(HALVES):
                    partial[mode, energy, target] = totals[target]
        return carry

    lax.fori_loop(0, energies // group, own_part, 0)

    for turn, far in chunks:
        for side in range(1, cores):
            send_side(turn, far, side).wait_recv()

    def send_out(to_half, to):
        turn = lax.rem(to_half - half + HALVES, HALVES)
        step = lax.rem(to - here + energies, energies)
        return pltpu.make_async_remote_copy(
            src_ref=result.at[to_half, to],
            dst_ref=landed.at[half, here],
            send_sem=out_send.at[turn, step],
            recv_sem=out_recv.at[turn, step],
            device_id=device(to, to_half, core),
            device_id_type=MESH,
        )

    order = sorted(range(group), key=lambda member: min(member, 1 + group - 1 - member))

    def one_group(index, carry):
        first = lax.rem(here // group + 1 + index, energies // group) * group
        sums = [[] for _ in range(modes)]
        for member in range(group):
            energy = first + order[member]
            for mode in range(modes):
                totals = [partial[mode, energy, target] for target in range(HALVES)]
                for side in range(1, cores):
                    totals = mix(aside.at[side - 1], energy, mode, side, totals)
                sums[mode].extend(totals)
        rights = []
        for mode in range(modes):
            high, low = split(jnp.concatenate(sums[mode], axis=0))
            rights.append(
                jnp.dot(
                    jnp.concatenate([high, low], axis=1), right_table[mode],
                    preferred_element_type=jnp.float32,
                )
            )
        for member in range(group):
            columns = []
            for target in range(HALVES):
                start = (member * HALVES + target) * rows
                stack = []
                for mode in range(modes):
                    block = rights[mode][start:start + rows]
                    high, low = split(jnp.concatenate([block, pltpu.roll(block, orbitals, 1)], axis=0))
                    stack += [high, low]
                columns.append(jnp.concatenate(stack, axis=0))
            product = jnp.dot(
                left_table[...], jnp.concatenate(columns, axis=1), preferred_element_type=jnp.float32
            )
            energy = first + order[member]
            for target in range(HALVES):
                both = product[:, target * lanes:(target + 1) * lanes]
                result[target, energy] = jnp.where(mask, both[:rows], both[rows:])
                own = jnp.logical_and(energy == here, half == target)

                @pl.when(jnp.logical_not(own))
                def _():
                    send_out(target, energy).start()

        return carry

    lax.fori_loop(0, energies // group, one_group, 0)
    landed[half, here] = result[half, here]

    for step in reversed(far_first):
        for turn in range(HALVES):
            if (turn, step) != (0, 0):
                send_out(around(half, turn, HALVES), around(here, step, energies)).wait_recv()
        pair = around(here, energies - step, energies)
        real, imag = landed[0, pair], landed[1, pair]
        out[0, 0, pair, pl.ds(0, rows), :] = jnp.where(mask, real, pltpu.roll(imag, orbitals, 1))
        out[0, 0, pair, pl.ds(rows, rows), :] = jnp.where(mask, pltpu.roll(real, orbitals, 1), imag)

    for turn, step in slots:
        if (turn, step) != (0, 0):
            send_in(turn, step).wait_send()
            send_out(around(half, turn, HALVES), around(here, step, energies)).wait_send()
    for turn, far in chunks:
        for side in range(1, cores):
            send_side(turn, far, side).wait_send()


def on_device(moms, energies, green_less, couplings, pair_atoms, shift_idx, weights):
    modes, orbitals = couplings.shape[1], couplings.shape[2]
    lanes, rows, cores = 2 * orbitals, orbitals // 2, moms // HALVES
    group = next(size for size in (4, 2, 1) if energies % size == 0)
    atoms_first = pair_atoms.T
    modes_first = weights.transpose(1, 0, 2)
    hbm = pl.BlockSpec(memory_space=pl.ANY)
    dma = pltpu.SemaphoreType.DMA
    return pl.pallas_call(
        functools.partial(kernel, (moms, energies, modes, orbitals, group)),
        out_shape=pltpu.VMEM(green_less.shape, jnp.float32),
        in_specs=[hbm] * 5,
        out_specs=pl.BlockSpec(memory_space=pltpu.VMEM),
        scratch_shapes=[
            pltpu.VMEM(green_less.shape, jnp.float32),
            pltpu.VMEM(couplings.shape, jnp.bfloat16),
            pltpu.SMEM(atoms_first.shape, jnp.int32),
            pltpu.SMEM(shift_idx.shape, jnp.int32),
            pltpu.SMEM(modes_first.shape, jnp.float32),
            pltpu.VMEM((HALVES, energies, rows, lanes), jnp.float32),
            pltpu.VMEM((HALVES, energies + 2 * SHIFT_MAX, rows, lanes), jnp.float32),
            pltpu.VMEM((cores - 1, HALVES, energies + 2 * SHIFT_MAX, rows, lanes), jnp.float32),
            pltpu.VMEM((modes, energies, HALVES, rows, lanes), jnp.float32),
            pltpu.VMEM((HALVES, energies, rows, lanes), jnp.float32),
            pltpu.VMEM((HALVES, energies, rows, lanes), jnp.float32),
            pltpu.VMEM((orbitals, modes * lanes), jnp.bfloat16),
            pltpu.VMEM((modes, 2 * lanes, lanes), jnp.bfloat16),
            dma((5,)),
            dma((HALVES, energies)),
            dma((HALVES, energies)),
            dma((cores, HALVES, 2)),
            dma((cores, HALVES, 2)),
            dma((HALVES, energies)),
            dma((HALVES, energies)),
        ],
        compiler_params=pltpu.CompilerParams(
            collective_id=0, has_side_effects=True, vmem_limit_bytes=58 * 2**20
        ),
    )(green_less, couplings, atoms_first, shift_idx, modes_first)


def solution(mesh):
    spec = P("mom", "energy", None, None, None)
    return jax.shard_map(
        functools.partial(on_device, mesh.shape["mom"], mesh.shape["energy"]),
        mesh=mesh,
        in_specs=(spec, P(), P(), P(), P()),
        out_specs=spec,
        check_vma=False,
    )
```

```python
import functools

import jax
import jax.numpy as jnp
from jax import lax
from jax.experimental import pallas as pl
from jax.experimental.pallas import tpu as pltpu
from jax.sharding import PartitionSpec as P

HALVES = 2
SHIFT_MAX = 4
MESH = pl.DeviceIdType.MESH


def split(value):
    high = value.astype(jnp.bfloat16)
    return high, (value - high.astype(jnp.float32)).astype(jnp.bfloat16)


def left_lanes(shape):
    return lax.broadcasted_iota(jnp.int32, shape, len(shape) - 1) < shape[-1] // 2


def iota(shape, axis):
    return lax.broadcasted_iota(jnp.int32, shape, axis)


def kernel(
    sizes,
    green_hbm, couplings_hbm, pair_atoms_hbm, shift_idx_hbm, weights_hbm,
    out,
    green, couplings, pair_atoms, shift_idx, weights, packed, held, aside, partial, result, landed, left_table, right_table,
    load_sem, in_send, in_recv, side_send, side_recv, out_send, out_recv,
):
    moms, energies, modes, orbitals, group = sizes
    reach = energies // 2
    lanes = 2 * orbitals
    rows = orbitals // 2
    cores = moms // HALVES
    here = lax.axis_index("energy")
    mom = lax.axis_index("mom")
    half, core = mom // cores, mom % cores

    def device(at, half_at, core_at):
        return (at, half_at * cores + core_at)

    def around(base, step, size):
        return lax.rem(base + step, size)

    barrier = pltpu.get_barrier_semaphore()
    for turn in range(HALVES):
        for step in range(1 if turn == 0 else 0, energies):
            pl.semaphore_signal(
                barrier, inc=1,
                device_id=device(around(here, step, energies), around(half, turn, HALVES), core),
                device_id_type=MESH,
            )
    for turn in range(1, cores):
        pl.semaphore_signal(
            barrier, inc=1, device_id=device(here, half, around(core, turn, cores)), device_id_type=MESH
        )

    load_green = pltpu.make_async_copy(green_hbm, green, load_sem.at[0])
    load_green.start()
    load_couplings = pltpu.make_async_copy(couplings_hbm, couplings, load_sem.at[1])
    load_couplings.start()
    load_small = [
        pltpu.make_async_copy(pair_atoms_hbm, pair_atoms, load_sem.at[2]),
        pltpu.make_async_copy(shift_idx_hbm, shift_idx, load_sem.at[3]),
        pltpu.make_async_copy(weights_hbm, weights, load_sem.at[4]),
    ]
    for load in load_small:
        load.start()

    edge = jnp.zeros((SHIFT_MAX, rows, lanes), jnp.float32)
    for source in range(HALVES):
        held[source, pl.ds(0, SHIFT_MAX)] = edge
        held[source, pl.ds(SHIFT_MAX + energies, SHIFT_MAX)] = edge
        for side in range(1, cores):
            aside[side - 1, source, pl.ds(0, SHIFT_MAX)] = edge
            aside[side - 1, source, pl.ds(SHIFT_MAX + energies, SHIFT_MAX)] = edge

    load_green.wait()
    mask = left_lanes((rows, lanes))
    for pair in range(energies):
        top = green[0, 0, pair, pl.ds(0, rows), :]
        bottom = green[0, 0, pair, pl.ds(rows, rows), :]
        packed[0, pair] = jnp.where(mask, top, pltpu.roll(bottom, orbitals, 1))
        packed[1, pair] = jnp.where(mask, pltpu.roll(top, orbitals, 1), bottom)

    pl.semaphore_wait(barrier, HALVES * energies - 1 + cores - 1)

    def send_in(turn, step):
        to_half, to = around(half, turn, HALVES), around(here, step, energies)
        return pltpu.make_async_remote_copy(
            src_ref=packed.at[to_half, to],
            dst_ref=held.at[half, SHIFT_MAX + here],
            send_sem=in_send.at[turn, step],
            recv_sem=in_recv.at[turn, here],
            device_id=device(to, to_half, core),
            device_id_type=MESH,
        )

    def send_side(turn, far, side):
        source = around(half, turn, HALVES)
        base = around(here // reach, far, energies // reach) * reach
        block = pl.ds(SHIFT_MAX + base, reach)
        return pltpu.make_async_remote_copy(
            src_ref=held.at[source, block],
            dst_ref=aside.at[side - 1, source, block],
            send_sem=side_send.at[side, turn, far],
            recv_sem=side_recv.at[side, turn, far],
            device_id=device(here, half, around(core, side, cores)),
            device_id_type=MESH,
        )

    def arrive_in(turn, source):
        def wait():
            slot = held.at[around(half, turn, HALVES), SHIFT_MAX + source]
            pltpu.make_async_remote_copy(
                src_ref=slot, dst_ref=slot, send_sem=in_send.at[turn, 0], recv_sem=in_recv.at[turn, source],
                device_id=device(here, half, around(core, 1, cores)), device_id_type=MESH,
            ).wait_recv()

        if turn == 0:
            pl.when(source != here)(wait)
        else:
            wait()

    far_first = sorted(range(energies), key=lambda step: -min(step, energies - step))
    slots = [(turn, step) for step in far_first for turn in range(HALVES)]
    near_first = slots[::-1]
    remote = [slot for slot in slots if slot != (0, 0)]
    for turn, step in remote:
        send_in(turn, step).start()

    held[half, SHIFT_MAX + here] = packed[half, here]

    load_couplings.wait()
    for load in load_small:
        load.wait()
    atom_a = pair_atoms[0, here]
    atom_b = pair_atoms[1, here]
    pick_same = (iota((orbitals, lanes), 0) == iota((orbitals, lanes), 1) % orbitals).astype(jnp.bfloat16)
    pick_other = (
        iota((orbitals, lanes), 0) == (iota((orbitals, lanes), 1) + rows) % orbitals
    ).astype(jnp.bfloat16)
    upper = iota((orbitals, lanes), 0) < rows
    same_block = (iota((lanes, lanes), 0) < orbitals) == (iota((lanes, lanes), 1) < orbitals)
    for mode in range(modes):
        left = couplings[atom_a, mode]
        right = couplings[atom_b, mode]
        left_same = jnp.dot(left, pick_same, preferred_element_type=jnp.float32)
        left_other = jnp.dot(left, pick_other, preferred_element_type=jnp.float32)
        left_table[:, pl.ds(mode * lanes, lanes)] = jnp.where(upper, left_same, left_other).astype(jnp.bfloat16)
        wide = lax.dot_general(
            right, pick_same, (((0,), (0,)), ((), ())), preferred_element_type=jnp.float32
        ).astype(jnp.bfloat16)
        tall = jnp.concatenate([wide, wide], axis=0)
        diagonal = jnp.where(same_block, tall.astype(jnp.float32), 0.0).astype(jnp.bfloat16)
        right_table[mode] = jnp.concatenate([diagonal, diagonal], axis=0)

    chunks = [(turn, far) for far in range(energies // reach) for turn in range(HALVES)]
    for turn, far in chunks:
        base = around(here // reach, far, energies // reach) * reach
        for member in range(reach):
            arrive_in(turn, base + member)
        for side in range(1, cores):
            send_side(turn, far, side).start()
    def mix(block, energy, mode, offset, totals):
        shift = shift_idx[mode]
        for row in range(HALVES):
            source = lax.rem(row + HALVES - (offset > core).astype(jnp.int32), HALVES)
            for sign, slot in ((0, energy - shift), (1, energy + shift)):
                value = block[source, SHIFT_MAX + slot]
                for target in range(HALVES):
                    turn = ((target - row) * cores + offset) % moms
                    term = weights[mode, sign, turn] * value
                    totals[target] = term if totals[target] is None else totals[target] + term
        return totals

    def own_part(index, carry):
        for member in range(group):
            energy = index * group + member
            for mode in range(modes):
                totals = mix(held, energy, mode, 0, [None] * HALVES)
                for target in range(HALVES):
                    partial[mode, energy, target] = totals[target]
        return carry

    lax.fori_loop(0, energies // group, own_part, 0)

    for turn, far in chunks:
        for side in range(1, cores):
            send_side(turn, far, side).wait_recv()

    def send_out(to_half, to):
        turn = lax.rem(to_half - half + HALVES, HALVES)
        step = lax.rem(to - here + energies, energies)
        return pltpu.make_async_remote_copy(
            src_ref=result.at[to_half, to],
            dst_ref=landed.at[half, here],
            send_sem=out_send.at[turn, step],
            recv_sem=out_recv.at[turn, step],
            device_id=device(to, to_half, core),
            device_id_type=MESH,
        )

    place = lax.rem(here, reach)

    def one_group(index, carry):
        chosen = [
            around(here // reach, 1 - side, 2) * reach + lax.rem(place + index + side, reach) for side in range(group)
        ]
        sums = [[] for _ in range(modes)]
        for energy in chosen:
            for mode in range(modes):
                totals = [partial[mode, energy, target] for target in range(HALVES)]
                for side in range(1, cores):
                    totals = mix(aside.at[side - 1], energy, mode, side, totals)
                sums[mode].extend(totals)
        rights = []
        for mode in range(modes):
            high, low = split(jnp.concatenate(sums[mode], axis=0))
            rights.append(
                jnp.dot(
                    jnp.concatenate([high, low], axis=1), right_table[mode],
                    preferred_element_type=jnp.float32,
                )
            )
        for member in range(group):
            columns = []
            for target in range(HALVES):
                start = (member * HALVES + target) * rows
                stack = []
                for mode in range(modes):
                    block = rights[mode][start:start + rows]
                    high, low = split(jnp.concatenate([block, pltpu.roll(block, orbitals, 1)], axis=0))
                    stack += [high, low]
                columns.append(jnp.concatenate(stack, axis=0))
            product = jnp.dot(
                left_table[...], jnp.concatenate(columns, axis=1), preferred_element_type=jnp.float32
            )
            energy = chosen[member]
            for target in range(HALVES):
                both = product[:, target * lanes:(target + 1) * lanes]
                result[target, energy] = jnp.where(mask, both[:rows], both[rows:])
                own = jnp.logical_and(energy == here, half == target)

                @pl.when(jnp.logical_not(own))
                def _():
                    send_out(target, energy).start()

        return carry

    lax.fori_loop(0, energies // group, one_group, 0)
    landed[half, here] = result[half, here]

    for step in reversed(far_first):
        for turn in range(HALVES):
            if (turn, step) != (0, 0):
                send_out(around(half, turn, HALVES), around(here, step, energies)).wait_recv()
        pair = around(here, energies - step, energies)
        real, imag = landed[0, pair], landed[1, pair]
        out[0, 0, pair, pl.ds(0, rows), :] = jnp.where(mask, real, pltpu.roll(imag, orbitals, 1))
        out[0, 0, pair, pl.ds(rows, rows), :] = jnp.where(mask, pltpu.roll(real, orbitals, 1), imag)

    for turn, step in slots:
        if (turn, step) != (0, 0):
            send_in(turn, step).wait_send()
            send_out(around(half, turn, HALVES), around(here, step, energies)).wait_send()
    for turn, far in chunks:
        for side in range(1, cores):
            send_side(turn, far, side).wait_send()


def on_device(moms, energies, green_less, couplings, pair_atoms, shift_idx, weights):
    modes, orbitals = couplings.shape[1], couplings.shape[2]
    lanes, rows, cores = 2 * orbitals, orbitals // 2, moms // HALVES
    group = 2
    atoms_first = pair_atoms.T
    modes_first = weights.transpose(1, 0, 2)
    hbm = pl.BlockSpec(memory_space=pl.ANY)
    dma = pltpu.SemaphoreType.DMA
    return pl.pallas_call(
        functools.partial(kernel, (moms, energies, modes, orbitals, group)),
        out_shape=pltpu.VMEM(green_less.shape, jnp.float32),
        in_specs=[hbm] * 5,
        out_specs=pl.BlockSpec(memory_space=pltpu.VMEM),
        scratch_shapes=[
            pltpu.VMEM(green_less.shape, jnp.float32),
            pltpu.VMEM(couplings.shape, jnp.bfloat16),
            pltpu.SMEM(atoms_first.shape, jnp.int32),
            pltpu.SMEM(shift_idx.shape, jnp.int32),
            pltpu.SMEM(modes_first.shape, jnp.float32),
            pltpu.VMEM((HALVES, energies, rows, lanes), jnp.float32),
            pltpu.VMEM((HALVES, energies + 2 * SHIFT_MAX, rows, lanes), jnp.float32),
            pltpu.VMEM((cores - 1, HALVES, energies + 2 * SHIFT_MAX, rows, lanes), jnp.float32),
            pltpu.VMEM((modes, energies, HALVES, rows, lanes), jnp.float32),
            pltpu.VMEM((HALVES, energies, rows, lanes), jnp.float32),
            pltpu.VMEM((HALVES, energies, rows, lanes), jnp.float32),
            pltpu.VMEM((orbitals, modes * lanes), jnp.bfloat16),
            pltpu.VMEM((modes, 2 * lanes, lanes), jnp.bfloat16),
            dma((5,)),
            dma((HALVES, energies)),
            dma((HALVES, energies)),
            dma((cores, HALVES, 2)),
            dma((cores, HALVES, 2)),
            dma((HALVES, energies)),
            dma((HALVES, energies)),
        ],
        compiler_params=pltpu.CompilerParams(
            collective_id=0, has_side_effects=True, vmem_limit_bytes=58 * 2**20
        ),
    )(green_less, couplings, atoms_first, shift_idx, modes_first)


def solution(mesh):
    spec = P("mom", "energy", None, None, None)
    return jax.shard_map(
        functools.partial(on_device, mesh.shape["mom"], mesh.shape["energy"]),
        mesh=mesh,
        in_specs=(spec, P(), P(), P(), P()),
        out_specs=spec,
        check_vma=False,
    )
```

```python
import functools

import jax
import jax.numpy as jnp
from jax import lax
from jax.experimental import pallas as pl
from jax.experimental.pallas import tpu as pltpu
from jax.sharding import PartitionSpec as P

HALVES = 2
SHIFT_MAX = 4
MESH = pl.DeviceIdType.MESH


def split(value):
    high = value.astype(jnp.bfloat16)
    return high, (value - high.astype(jnp.float32)).astype(jnp.bfloat16)


def left_lanes(shape):
    return lax.broadcasted_iota(jnp.int32, shape, len(shape) - 1) < shape[-1] // 2


def iota(shape, axis):
    return lax.broadcasted_iota(jnp.int32, shape, axis)


def kernel(
    sizes,
    green_hbm, couplings_hbm, pair_atoms_hbm, shift_idx_hbm, weights_hbm,
    out,
    green, couplings, pair_atoms, shift_idx, weights, packed, held, aside, partial, result, landed, left_table, right_table,
    load_sem, in_send, in_recv, side_send, side_recv, out_send, out_recv,
):
    moms, energies, modes, orbitals, group = sizes
    reach = energies // 2
    lanes = 2 * orbitals
    rows = orbitals // 2
    cores = moms // HALVES
    here = lax.axis_index("energy")
    mom = lax.axis_index("mom")
    half, core = mom // cores, mom % cores

    def device(at, half_at, core_at):
        return (at, half_at * cores + core_at)

    def around(base, step, size):
        return lax.rem(base + step, size)

    barrier = pltpu.get_barrier_semaphore()
    for turn in range(HALVES):
        for step in range(1 if turn == 0 else 0, energies):
            pl.semaphore_signal(
                barrier, inc=1,
                device_id=device(around(here, step, energies), around(half, turn, HALVES), core),
                device_id_type=MESH,
            )
    for turn in range(1, cores):
        pl.semaphore_signal(
            barrier, inc=1, device_id=device(here, half, around(core, turn, cores)), device_id_type=MESH
        )

    load_green = pltpu.make_async_copy(green_hbm, green, load_sem.at[0])
    load_green.start()
    edge = jnp.zeros((SHIFT_MAX, rows, lanes), jnp.float32)
    for source in range(HALVES):
        held[source, pl.ds(0, SHIFT_MAX)] = edge
        held[source, pl.ds(SHIFT_MAX + energies, SHIFT_MAX)] = edge
        for side in range(1, cores):
            aside[side - 1, source, pl.ds(0, SHIFT_MAX)] = edge
            aside[side - 1, source, pl.ds(SHIFT_MAX + energies, SHIFT_MAX)] = edge

    load_green.wait()
    load_couplings = pltpu.make_async_copy(couplings_hbm, couplings, load_sem.at[1])
    load_couplings.start()
    load_small = [
        pltpu.make_async_copy(pair_atoms_hbm, pair_atoms, load_sem.at[2]),
        pltpu.make_async_copy(shift_idx_hbm, shift_idx, load_sem.at[3]),
        pltpu.make_async_copy(weights_hbm, weights, load_sem.at[4]),
    ]
    for load in load_small:
        load.start()
    mask = left_lanes((rows, lanes))
    for pair in range(energies):
        top = green[0, 0, pair, pl.ds(0, rows), :]
        bottom = green[0, 0, pair, pl.ds(rows, rows), :]
        packed[0, pair] = jnp.where(mask, top, pltpu.roll(bottom, orbitals, 1))
        packed[1, pair] = jnp.where(mask, pltpu.roll(top, orbitals, 1), bottom)

    pl.semaphore_wait(barrier, HALVES * energies - 1 + cores - 1)

    def send_in(turn, step):
        to_half, to = around(half, turn, HALVES), around(here, step, energies)
        return pltpu.make_async_remote_copy(
            src_ref=packed.at[to_half, to],
            dst_ref=held.at[half, SHIFT_MAX + here],
            send_sem=in_send.at[turn, step],
            recv_sem=in_recv.at[turn, here],
            device_id=device(to, to_half, core),
            device_id_type=MESH,
        )

    piece = reach // 2

    def base_of(part):
        return around(here // reach, part // 2, 2) * reach + part % 2 * piece

    def send_side(turn, part, side):
        source = around(half, turn, HALVES)
        block = pl.ds(SHIFT_MAX + base_of(part), piece)
        return pltpu.make_async_remote_copy(
            src_ref=held.at[source, block],
            dst_ref=aside.at[side - 1, source, block],
            send_sem=side_send.at[side, turn, part],
            recv_sem=side_recv.at[side, turn, part],
            device_id=device(here, half, around(core, side, cores)),
            device_id_type=MESH,
        )

    def arrive_in(turn, source):
        def wait():
            slot = held.at[around(half, turn, HALVES), SHIFT_MAX + source]
            pltpu.make_async_remote_copy(
                src_ref=slot, dst_ref=slot, send_sem=in_send.at[turn, 0], recv_sem=in_recv.at[turn, source],
                device_id=device(here, half, around(core, 1, cores)), device_id_type=MESH,
            ).wait_recv()

        if turn == 0:
            pl.when(source != here)(wait)
        else:
            wait()

    far_first = sorted(range(energies), key=lambda step: -min(step, energies - step))
    slots = [(turn, step) for step in far_first for turn in range(HALVES)]
    near_first = slots[::-1]
    place = lax.rem(here, reach)
    for index in range(reach):
        for side in range(2):
            to = around(here // reach, 1 - side, 2) * reach + lax.rem(place + index + side, reach)
            for turn in range(HALVES):
                if (turn, side, index) != (0, 1, reach - 1):
                    send_in(turn, lax.rem(to - here + energies, energies)).start()

    held[half, SHIFT_MAX + here] = packed[half, here]

    load_couplings.wait()
    for load in load_small:
        load.wait()
    atom_a = pair_atoms[0, here]
    atom_b = pair_atoms[1, here]
    pick_same = (iota((orbitals, lanes), 0) == iota((orbitals, lanes), 1) % orbitals).astype(jnp.bfloat16)
    pick_other = (
        iota((orbitals, lanes), 0) == (iota((orbitals, lanes), 1) + rows) % orbitals
    ).astype(jnp.bfloat16)
    upper = iota((orbitals, lanes), 0) < rows
    same_block = (iota((lanes, lanes), 0) < orbitals) == (iota((lanes, lanes), 1) < orbitals)
    for mode in range(modes):
        left = couplings[atom_a, mode]
        right = couplings[atom_b, mode]
        left_same = jnp.dot(left, pick_same, preferred_element_type=jnp.float32)
        left_other = jnp.dot(left, pick_other, preferred_element_type=jnp.float32)
        left_table[:, pl.ds(mode * lanes, lanes)] = jnp.where(upper, left_same, left_other).astype(jnp.bfloat16)
        wide = lax.dot_general(
            right, pick_same, (((0,), (0,)), ((), ())), preferred_element_type=jnp.float32
        ).astype(jnp.bfloat16)
        tall = jnp.concatenate([wide, wide], axis=0)
        diagonal = jnp.where(same_block, tall.astype(jnp.float32), 0.0).astype(jnp.bfloat16)
        right_table[mode] = jnp.concatenate([diagonal, diagonal], axis=0)

    chunks = [(turn, part) for part in range(energies // piece) for turn in range(HALVES)]
    for turn, part in chunks:
        for member in range(piece):
            arrive_in(turn, base_of(part) + member)
        for side in range(1, cores):
            send_side(turn, part, side).start()
    def mix(block, energy, mode, offset, totals):
        shift = shift_idx[mode]
        for row in range(HALVES):
            source = lax.rem(row + HALVES - (offset > core).astype(jnp.int32), HALVES)
            for sign, slot in ((0, energy - shift), (1, energy + shift)):
                value = block[source, SHIFT_MAX + slot]
                for target in range(HALVES):
                    turn = ((target - row) * cores + offset) % moms
                    term = weights[mode, sign, turn] * value
                    totals[target] = term if totals[target] is None else totals[target] + term
        return totals

    def own_part(index, carry):
        for member in range(group):
            energy = index * group + member
            for mode in range(modes):
                totals = mix(held, energy, mode, 0, [None] * HALVES)
                for target in range(HALVES):
                    partial[mode, energy, target] = totals[target]
        return carry

    lax.fori_loop(0, energies // group, own_part, 0)

    for turn, part in chunks:
        for side in range(1, cores):
            send_side(turn, part, side).wait_recv()

    def send_out(to_half, to):
        turn = lax.rem(to_half - half + HALVES, HALVES)
        step = lax.rem(to - here + energies, energies)
        return pltpu.make_async_remote_copy(
            src_ref=result.at[to_half, to],
            dst_ref=landed.at[half, here],
            send_sem=out_send.at[turn, step],
            recv_sem=out_recv.at[turn, step],
            device_id=device(to, to_half, core),
            device_id_type=MESH,
        )

    def one_group(index, carry):
        chosen = [
            around(here // reach, 1 - side, 2) * reach + lax.rem(place + index + side, reach) for side in range(group)
        ]
        sums = [[] for _ in range(modes)]
        for energy in chosen:
            for mode in range(modes):
                totals = [partial[mode, energy, target] for target in range(HALVES)]
                for side in range(1, cores):
                    totals = mix(aside.at[side - 1], energy, mode, side, totals)
                sums[mode].extend(totals)
        rights = []
        for mode in range(modes):
            high, low = split(jnp.concatenate(sums[mode], axis=0))
            rights.append(
                jnp.dot(
                    jnp.concatenate([high, low], axis=1), right_table[mode],
                    preferred_element_type=jnp.float32,
                )
            )
        for member in range(group):
            columns = []
            for target in range(HALVES):
                start = (member * HALVES + target) * rows
                stack = []
                for mode in range(modes):
                    block = rights[mode][start:start + rows]
                    high, low = split(jnp.concatenate([block, pltpu.roll(block, orbitals, 1)], axis=0))
                    stack += [high, low]
                columns.append(jnp.concatenate(stack, axis=0))
            product = jnp.dot(
                left_table[...], jnp.concatenate(columns, axis=1), preferred_element_type=jnp.float32
            )
            energy = chosen[member]
            for target in range(HALVES):
                both = product[:, target * lanes:(target + 1) * lanes]
                result[target, energy] = jnp.where(mask, both[:rows], both[rows:])
                own = jnp.logical_and(energy == here, half == target)

                @pl.when(jnp.logical_not(own))
                def _():
                    send_out(target, energy).start()

        return carry

    lax.fori_loop(0, energies // group, one_group, 0)
    landed[half, here] = result[half, here]

    for step in reversed(far_first):
        for turn in range(HALVES):
            if (turn, step) != (0, 0):
                send_out(around(half, turn, HALVES), around(here, step, energies)).wait_recv()
        pair = around(here, energies - step, energies)
        real, imag = landed[0, pair], landed[1, pair]
        out[0, 0, pair, pl.ds(0, rows), :] = jnp.where(mask, real, pltpu.roll(imag, orbitals, 1))
        out[0, 0, pair, pl.ds(rows, rows), :] = jnp.where(mask, pltpu.roll(real, orbitals, 1), imag)

    for turn, step in slots:
        if (turn, step) != (0, 0):
            send_in(turn, step).wait_send()
            send_out(around(half, turn, HALVES), around(here, step, energies)).wait_send()
    for turn, part in chunks:
        for side in range(1, cores):
            send_side(turn, part, side).wait_send()


def on_device(moms, energies, green_less, couplings, pair_atoms, shift_idx, weights):
    modes, orbitals = couplings.shape[1], couplings.shape[2]
    lanes, rows, cores = 2 * orbitals, orbitals // 2, moms // HALVES
    group = 2
    atoms_first = pair_atoms.T
    modes_first = weights.transpose(1, 0, 2)
    hbm = pl.BlockSpec(memory_space=pl.ANY)
    dma = pltpu.SemaphoreType.DMA
    return pl.pallas_call(
        functools.partial(kernel, (moms, energies, modes, orbitals, group)),
        out_shape=pltpu.VMEM(green_less.shape, jnp.float32),
        in_specs=[hbm] * 5,
        out_specs=pl.BlockSpec(memory_space=pltpu.VMEM),
        scratch_shapes=[
            pltpu.VMEM(green_less.shape, jnp.float32),
            pltpu.VMEM(couplings.shape, jnp.bfloat16),
            pltpu.SMEM(atoms_first.shape, jnp.int32),
            pltpu.SMEM(shift_idx.shape, jnp.int32),
            pltpu.SMEM(modes_first.shape, jnp.float32),
            pltpu.VMEM((HALVES, energies, rows, lanes), jnp.float32),
            pltpu.VMEM((HALVES, energies + 2 * SHIFT_MAX, rows, lanes), jnp.float32),
            pltpu.VMEM((cores - 1, HALVES, energies + 2 * SHIFT_MAX, rows, lanes), jnp.float32),
            pltpu.VMEM((modes, energies, HALVES, rows, lanes), jnp.float32),
            pltpu.VMEM((HALVES, energies, rows, lanes), jnp.float32),
            pltpu.VMEM((HALVES, energies, rows, lanes), jnp.float32),
            pltpu.VMEM((orbitals, modes * lanes), jnp.bfloat16),
            pltpu.VMEM((modes, 2 * lanes, lanes), jnp.bfloat16),
            dma((5,)),
            dma((HALVES, energies)),
            dma((HALVES, energies)),
            dma((cores, HALVES, 4)),
            dma((cores, HALVES, 4)),
            dma((HALVES, energies)),
            dma((HALVES, energies)),
        ],
        compiler_params=pltpu.CompilerParams(
            collective_id=0, has_side_effects=True, vmem_limit_bytes=58 * 2**20
        ),
    )(green_less, couplings, atoms_first, shift_idx, modes_first)


def solution(mesh):
    spec = P("mom", "energy", None, None, None)
    return jax.shard_map(
        functools.partial(on_device, mesh.shape["mom"], mesh.shape["energy"]),
        mesh=mesh,
        in_specs=(spec, P(), P(), P(), P()),
        out_specs=spec,
        check_vma=False,
    )
```

```python
import functools

import jax
import jax.numpy as jnp
from jax import lax
from jax.experimental import pallas as pl
from jax.experimental.pallas import tpu as pltpu
from jax.sharding import PartitionSpec as P

HALVES = 2
SHIFT_MAX = 4
MESH = pl.DeviceIdType.MESH


def split(value):
    high = value.astype(jnp.bfloat16)
    return high, (value - high.astype(jnp.float32)).astype(jnp.bfloat16)


def left_lanes(shape):
    return lax.broadcasted_iota(jnp.int32, shape, len(shape) - 1) < shape[-1] // 2


def iota(shape, axis):
    return lax.broadcasted_iota(jnp.int32, shape, axis)


def kernel(
    sizes,
    green_hbm, couplings_hbm, pair_atoms_hbm, shift_idx_hbm, weights_hbm,
    out,
    green, couplings, pair_atoms, shift_idx, weights, packed, held, aside, partial, result, landed, left_table, right_table,
    load_sem, in_send, in_recv, side_send, side_recv, out_send, out_recv,
):
    moms, energies, modes, orbitals, group = sizes
    reach = energies // 2
    lanes = 2 * orbitals
    rows = orbitals // 2
    cores = moms // HALVES
    here = lax.axis_index("energy")
    mom = lax.axis_index("mom")
    half, core = mom // cores, mom % cores

    def device(at, half_at, core_at):
        return (at, half_at * cores + core_at)

    def around(base, step, size):
        return lax.rem(base + step, size)

    barrier = pltpu.get_barrier_semaphore()
    for turn in range(HALVES):
        for step in range(1 if turn == 0 else 0, energies):
            pl.semaphore_signal(
                barrier, inc=1,
                device_id=device(around(here, step, energies), around(half, turn, HALVES), core),
                device_id_type=MESH,
            )
    for turn in range(1, cores):
        pl.semaphore_signal(
            barrier, inc=1, device_id=device(here, half, around(core, turn, cores)), device_id_type=MESH
        )

    load_green = pltpu.make_async_copy(green_hbm, green, load_sem.at[0])
    load_green.start()
    edge = jnp.zeros((SHIFT_MAX, rows, lanes), jnp.float32)
    for source in range(HALVES):
        held[source, pl.ds(0, SHIFT_MAX)] = edge
        held[source, pl.ds(SHIFT_MAX + energies, SHIFT_MAX)] = edge
        for side in range(1, cores):
            aside[side - 1, source, pl.ds(0, SHIFT_MAX)] = edge
            aside[side - 1, source, pl.ds(SHIFT_MAX + energies, SHIFT_MAX)] = edge

    load_green.wait()
    load_couplings = pltpu.make_async_copy(couplings_hbm, couplings, load_sem.at[1])
    load_couplings.start()
    load_small = [
        pltpu.make_async_copy(pair_atoms_hbm, pair_atoms, load_sem.at[2]),
        pltpu.make_async_copy(shift_idx_hbm, shift_idx, load_sem.at[3]),
        pltpu.make_async_copy(weights_hbm, weights, load_sem.at[4]),
    ]
    for load in load_small:
        load.start()
    mask = left_lanes((rows, lanes))
    for pair in range(energies):
        top = green[0, 0, pair, pl.ds(0, rows), :]
        bottom = green[0, 0, pair, pl.ds(rows, rows), :]
        packed[0, pair] = jnp.where(mask, top, pltpu.roll(bottom, orbitals, 1))
        packed[1, pair] = jnp.where(mask, pltpu.roll(top, orbitals, 1), bottom)

    pl.semaphore_wait(barrier, HALVES * energies - 1 + cores - 1)

    def send_in(turn, step):
        to_half, to = around(half, turn, HALVES), around(here, step, energies)
        return pltpu.make_async_remote_copy(
            src_ref=packed.at[to_half, to],
            dst_ref=held.at[half, SHIFT_MAX + here],
            send_sem=in_send.at[turn, step],
            recv_sem=in_recv.at[turn, here],
            device_id=device(to, to_half, core),
            device_id_type=MESH,
        )

    def send_side(turn, far, side):
        source = around(half, turn, HALVES)
        base = around(here // reach, far, energies // reach) * reach
        block = pl.ds(SHIFT_MAX + base, reach)
        return pltpu.make_async_remote_copy(
            src_ref=held.at[source, block],
            dst_ref=aside.at[side - 1, source, block],
            send_sem=side_send.at[side, turn, far],
            recv_sem=side_recv.at[side, turn, far],
            device_id=device(here, half, around(core, side, cores)),
            device_id_type=MESH,
        )

    def arrive_in(turn, source):
        def wait():
            slot = held.at[around(half, turn, HALVES), SHIFT_MAX + source]
            pltpu.make_async_remote_copy(
                src_ref=slot, dst_ref=slot, send_sem=in_send.at[turn, 0], recv_sem=in_recv.at[turn, source],
                device_id=device(here, half, around(core, 1, cores)), device_id_type=MESH,
            ).wait_recv()

        if turn == 0:
            pl.when(source != here)(wait)
        else:
            wait()

    far_first = sorted(range(energies), key=lambda step: -min(step, energies - step))
    slots = [(turn, step) for step in far_first for turn in range(HALVES)]
    near_first = slots[::-1]
    remote = [slot for slot in slots if slot != (0, 0)]
    for turn, step in remote:
        send_in(turn, step).start()

    held[half, SHIFT_MAX + here] = packed[half, here]

    load_couplings.wait()
    for load in load_small:
        load.wait()
    atom_a = pair_atoms[0, here]
    atom_b = pair_atoms[1, here]
    pick_same = (iota((orbitals, lanes), 0) == iota((orbitals, lanes), 1) % orbitals).astype(jnp.bfloat16)
    pick_other = (
        iota((orbitals, lanes), 0) == (iota((orbitals, lanes), 1) + rows) % orbitals
    ).astype(jnp.bfloat16)
    upper = iota((orbitals, lanes), 0) < rows
    same_block = (iota((lanes, lanes), 0) < orbitals) == (iota((lanes, lanes), 1) < orbitals)
    for mode in range(modes):
        left = couplings[atom_a, mode]
        right = couplings[atom_b, mode]
        left_same = jnp.dot(left, pick_same, preferred_element_type=jnp.float32)
        left_other = jnp.dot(left, pick_other, preferred_element_type=jnp.float32)
        left_table[:, pl.ds(mode * lanes, lanes)] = jnp.where(upper, left_same, left_other).astype(jnp.bfloat16)
        wide = lax.dot_general(
            right, pick_same, (((0,), (0,)), ((), ())), preferred_element_type=jnp.float32
        ).astype(jnp.bfloat16)
        tall = jnp.concatenate([wide, wide], axis=0)
        diagonal = jnp.where(same_block, tall.astype(jnp.float32), 0.0).astype(jnp.bfloat16)
        right_table[mode] = jnp.concatenate([diagonal, diagonal], axis=0)

    chunks = [(turn, far) for far in range(energies // reach) for turn in range(HALVES)]
    for turn, far in chunks:
        base = around(here // reach, far, energies // reach) * reach
        for member in range(reach):
            arrive_in(turn, base + member)
        for side in range(1, cores):
            send_side(turn, far, side).start()
    def mix(block, energy, mode, offset, totals):
        shift = shift_idx[mode]
        for row in range(HALVES):
            source = lax.rem(row + HALVES - (offset > core).astype(jnp.int32), HALVES)
            for sign, slot in ((0, energy - shift), (1, energy + shift)):
                value = block[source, SHIFT_MAX + slot]
                for target in range(HALVES):
                    turn = ((target - row) * cores + offset) % moms
                    term = weights[mode, sign, turn] * value
                    totals[target] = term if totals[target] is None else totals[target] + term
        return totals

    def own_part(index, carry):
        for member in range(group):
            energy = index * group + member
            for mode in range(modes):
                totals = mix(held, energy, mode, 0, [None] * HALVES)
                for target in range(HALVES):
                    partial[mode, energy, target] = totals[target]
        return carry

    lax.fori_loop(0, energies // group, own_part, 0)

    for turn, far in chunks:
        for side in range(1, cores):
            send_side(turn, far, side).wait_recv()

    def send_out(to_half, to):
        turn = lax.rem(to_half - half + HALVES, HALVES)
        step = lax.rem(to - here + energies, energies)
        return pltpu.make_async_remote_copy(
            src_ref=result.at[to_half, to],
            dst_ref=landed.at[half, here],
            send_sem=out_send.at[turn, step],
            recv_sem=out_recv.at[turn, step],
            device_id=device(to, to_half, core),
            device_id_type=MESH,
        )

    upper = here // reach

    def one_group(index, carry):
        chosen = [
            upper * (group * index + member) + (1 - upper) * (index + member * reach) for member in range(group)
        ]
        sums = [[] for _ in range(modes)]
        for energy in chosen:
            for mode in range(modes):
                totals = [partial[mode, energy, target] for target in range(HALVES)]
                for side in range(1, cores):
                    totals = mix(aside.at[side - 1], energy, mode, side, totals)
                sums[mode].extend(totals)
        rights = []
        for mode in range(modes):
            high, low = split(jnp.concatenate(sums[mode], axis=0))
            rights.append(
                jnp.dot(
                    jnp.concatenate([high, low], axis=1), right_table[mode],
                    preferred_element_type=jnp.float32,
                )
            )
        for member in range(group):
            columns = []
            for target in range(HALVES):
                start = (member * HALVES + target) * rows
                stack = []
                for mode in range(modes):
                    block = rights[mode][start:start + rows]
                    high, low = split(jnp.concatenate([block, pltpu.roll(block, orbitals, 1)], axis=0))
                    stack += [high, low]
                columns.append(jnp.concatenate(stack, axis=0))
            product = jnp.dot(
                left_table[...], jnp.concatenate(columns, axis=1), preferred_element_type=jnp.float32
            )
            energy = chosen[member]
            for target in range(HALVES):
                both = product[:, target * lanes:(target + 1) * lanes]
                result[target, energy] = jnp.where(mask, both[:rows], both[rows:])
                own = jnp.logical_and(energy == here, half == target)

                @pl.when(jnp.logical_not(own))
                def _():
                    send_out(target, energy).start()

        return carry

    lax.fori_loop(0, energies // group, one_group, 0)
    landed[half, here] = result[half, here]

    for step in reversed(far_first):
        for turn in range(HALVES):
            if (turn, step) != (0, 0):
                send_out(around(half, turn, HALVES), around(here, step, energies)).wait_recv()
        pair = around(here, energies - step, energies)
        real, imag = landed[0, pair], landed[1, pair]
        out[0, 0, pair, pl.ds(0, rows), :] = jnp.where(mask, real, pltpu.roll(imag, orbitals, 1))
        out[0, 0, pair, pl.ds(rows, rows), :] = jnp.where(mask, pltpu.roll(real, orbitals, 1), imag)

    for turn, step in slots:
        if (turn, step) != (0, 0):
            send_in(turn, step).wait_send()
            send_out(around(half, turn, HALVES), around(here, step, energies)).wait_send()
    for turn, far in chunks:
        for side in range(1, cores):
            send_side(turn, far, side).wait_send()


def on_device(moms, energies, green_less, couplings, pair_atoms, shift_idx, weights):
    modes, orbitals = couplings.shape[1], couplings.shape[2]
    lanes, rows, cores = 2 * orbitals, orbitals // 2, moms // HALVES
    group = 2
    atoms_first = pair_atoms.T
    modes_first = weights.transpose(1, 0, 2)
    hbm = pl.BlockSpec(memory_space=pl.ANY)
    dma = pltpu.SemaphoreType.DMA
    return pl.pallas_call(
        functools.partial(kernel, (moms, energies, modes, orbitals, group)),
        out_shape=pltpu.VMEM(green_less.shape, jnp.float32),
        in_specs=[hbm] * 5,
        out_specs=pl.BlockSpec(memory_space=pltpu.VMEM),
        scratch_shapes=[
            pltpu.VMEM(green_less.shape, jnp.float32),
            pltpu.VMEM(couplings.shape, jnp.bfloat16),
            pltpu.SMEM(atoms_first.shape, jnp.int32),
            pltpu.SMEM(shift_idx.shape, jnp.int32),
            pltpu.SMEM(modes_first.shape, jnp.float32),
            pltpu.VMEM((HALVES, energies, rows, lanes), jnp.float32),
            pltpu.VMEM((HALVES, energies + 2 * SHIFT_MAX, rows, lanes), jnp.float32),
            pltpu.VMEM((cores - 1, HALVES, energies + 2 * SHIFT_MAX, rows, lanes), jnp.float32),
            pltpu.VMEM((modes, energies, HALVES, rows, lanes), jnp.float32),
            pltpu.VMEM((HALVES, energies, rows, lanes), jnp.float32),
            pltpu.VMEM((HALVES, energies, rows, lanes), jnp.float32),
            pltpu.VMEM((orbitals, modes * lanes), jnp.bfloat16),
            pltpu.VMEM((modes, 2 * lanes, lanes), jnp.bfloat16),
            dma((5,)),
            dma((HALVES, energies)),
            dma((HALVES, energies)),
            dma((cores, HALVES, 2)),
            dma((cores, HALVES, 2)),
            dma((HALVES, energies)),
            dma((HALVES, energies)),
        ],
        compiler_params=pltpu.CompilerParams(
            collective_id=0, has_side_effects=True, vmem_limit_bytes=58 * 2**20
        ),
    )(green_less, couplings, atoms_first, shift_idx, modes_first)


def solution(mesh):
    spec = P("mom", "energy", None, None, None)
    return jax.shard_map(
        functools.partial(on_device, mesh.shape["mom"], mesh.shape["energy"]),
        mesh=mesh,
        in_specs=(spec, P(), P(), P(), P()),
        out_specs=spec,
        check_vma=False,
    )
```

```python
import functools

import jax
import jax.numpy as jnp
from jax import lax
from jax.experimental import pallas as pl
from jax.experimental.pallas import tpu as pltpu
from jax.sharding import PartitionSpec as P

HALVES = 2
SHIFT_MAX = 4
MESH = pl.DeviceIdType.MESH


def split(value):
    high = value.astype(jnp.bfloat16)
    return high, (value - high.astype(jnp.float32)).astype(jnp.bfloat16)


def left_lanes(shape):
    return lax.broadcasted_iota(jnp.int32, shape, len(shape) - 1) < shape[-1] // 2


def iota(shape, axis):
    return lax.broadcasted_iota(jnp.int32, shape, axis)


def kernel(
    sizes,
    green_hbm, couplings_hbm, pair_atoms_hbm, shift_idx_hbm, weights_hbm,
    out,
    green, couplings, pair_atoms, shift_idx, weights, packed, held, aside, partial, result, landed, left_table, right_table,
    load_sem, in_send, in_recv, side_send, side_recv, out_send, out_recv,
):
    moms, energies, modes, orbitals, group = sizes
    reach = energies // 2
    lanes = 2 * orbitals
    rows = orbitals // 2
    cores = moms // HALVES
    here = lax.axis_index("energy")
    mom = lax.axis_index("mom")
    half, core = mom // cores, mom % cores

    def device(at, half_at, core_at):
        return (at, half_at * cores + core_at)

    def around(base, step, size):
        return lax.rem(base + step, size)

    barrier = pltpu.get_barrier_semaphore()
    for turn in range(HALVES):
        for step in range(1 if turn == 0 else 0, energies):
            pl.semaphore_signal(
                barrier, inc=1,
                device_id=device(around(here, step, energies), around(half, turn, HALVES), core),
                device_id_type=MESH,
            )
    for turn in range(1, cores):
        pl.semaphore_signal(
            barrier, inc=1, device_id=device(here, half, around(core, turn, cores)), device_id_type=MESH
        )

    load_green = pltpu.make_async_copy(green_hbm, green, load_sem.at[0])
    load_green.start()
    edge = jnp.zeros((SHIFT_MAX, rows, lanes), jnp.float32)
    for source in range(HALVES):
        held[source, pl.ds(0, SHIFT_MAX)] = edge
        held[source, pl.ds(SHIFT_MAX + energies, SHIFT_MAX)] = edge
        for side in range(1, cores):
            aside[side - 1, source, pl.ds(0, SHIFT_MAX)] = edge
            aside[side - 1, source, pl.ds(SHIFT_MAX + energies, SHIFT_MAX)] = edge

    load_green.wait()
    load_couplings = pltpu.make_async_copy(couplings_hbm, couplings, load_sem.at[1])
    load_couplings.start()
    load_small = [
        pltpu.make_async_copy(pair_atoms_hbm, pair_atoms, load_sem.at[2]),
        pltpu.make_async_copy(shift_idx_hbm, shift_idx, load_sem.at[3]),
        pltpu.make_async_copy(weights_hbm, weights, load_sem.at[4]),
    ]
    for load in load_small:
        load.start()
    mask = left_lanes((rows, lanes))
    for pair in range(energies):
        top = green[0, 0, pair, pl.ds(0, rows), :]
        bottom = green[0, 0, pair, pl.ds(rows, rows), :]
        packed[0, pair] = jnp.where(mask, top, pltpu.roll(bottom, orbitals, 1))
        packed[1, pair] = jnp.where(mask, pltpu.roll(top, orbitals, 1), bottom)

    pl.semaphore_wait(barrier, HALVES * energies - 1 + cores - 1)

    def send_in(turn, step):
        to_half, to = around(half, turn, HALVES), around(here, step, energies)
        return pltpu.make_async_remote_copy(
            src_ref=packed.at[to_half, to],
            dst_ref=held.at[half, SHIFT_MAX + here],
            send_sem=in_send.at[turn, step],
            recv_sem=in_recv.at[turn, here],
            device_id=device(to, to_half, core),
            device_id_type=MESH,
        )

    piece = reach // 2

    def base_of(part):
        return around(here // reach, part // 2, 2) * reach + part % 2 * piece

    def send_side(turn, part, side):
        source = around(half, turn, HALVES)
        block = pl.ds(SHIFT_MAX + base_of(part), piece)
        return pltpu.make_async_remote_copy(
            src_ref=held.at[source, block],
            dst_ref=aside.at[side - 1, source, block],
            send_sem=side_send.at[side, turn, part],
            recv_sem=side_recv.at[side, turn, part],
            device_id=device(here, half, around(core, side, cores)),
            device_id_type=MESH,
        )

    def arrive_in(turn, source):
        def wait():
            slot = held.at[around(half, turn, HALVES), SHIFT_MAX + source]
            pltpu.make_async_remote_copy(
                src_ref=slot, dst_ref=slot, send_sem=in_send.at[turn, 0], recv_sem=in_recv.at[turn, source],
                device_id=device(here, half, around(core, 1, cores)), device_id_type=MESH,
            ).wait_recv()

        if turn == 0:
            pl.when(source != here)(wait)
        else:
            wait()

    far_first = sorted(range(energies), key=lambda step: -min(step, energies - step))
    slots = [(turn, step) for step in far_first for turn in range(HALVES)]
    near_first = slots[::-1]
    remote = [slot for slot in slots if slot != (0, 0)]
    for turn, step in remote:
        send_in(turn, step).start()

    held[half, SHIFT_MAX + here] = packed[half, here]

    load_couplings.wait()
    for load in load_small:
        load.wait()
    atom_a = pair_atoms[0, here]
    atom_b = pair_atoms[1, here]
    pick_same = (iota((orbitals, lanes), 0) == iota((orbitals, lanes), 1) % orbitals).astype(jnp.bfloat16)
    pick_other = (
        iota((orbitals, lanes), 0) == (iota((orbitals, lanes), 1) + rows) % orbitals
    ).astype(jnp.bfloat16)
    upper = iota((orbitals, lanes), 0) < rows
    same_block = (iota((lanes, lanes), 0) < orbitals) == (iota((lanes, lanes), 1) < orbitals)
    for mode in range(modes):
        left = couplings[atom_a, mode]
        right = couplings[atom_b, mode]
        left_same = jnp.dot(left, pick_same, preferred_element_type=jnp.float32)
        left_other = jnp.dot(left, pick_other, preferred_element_type=jnp.float32)
        left_table[:, pl.ds(mode * lanes, lanes)] = jnp.where(upper, left_same, left_other).astype(jnp.bfloat16)
        wide = lax.dot_general(
            right, pick_same, (((0,), (0,)), ((), ())), preferred_element_type=jnp.float32
        ).astype(jnp.bfloat16)
        tall = jnp.concatenate([wide, wide], axis=0)
        diagonal = jnp.where(same_block, tall.astype(jnp.float32), 0.0).astype(jnp.bfloat16)
        right_table[mode] = jnp.concatenate([diagonal, diagonal], axis=0)

    chunks = [(turn, part) for part in range(energies // piece) for turn in range(HALVES)]
    for turn, part in chunks:
        for member in range(piece):
            arrive_in(turn, base_of(part) + member)
        for side in range(1, cores):
            send_side(turn, part, side).start()
    def mix(block, energy, mode, offset, totals):
        shift = shift_idx[mode]
        for row in range(HALVES):
            source = lax.rem(row + HALVES - (offset > core).astype(jnp.int32), HALVES)
            for sign, slot in ((0, energy - shift), (1, energy + shift)):
                value = block[source, SHIFT_MAX + slot]
                for target in range(HALVES):
                    turn = ((target - row) * cores + offset) % moms
                    term = weights[mode, sign, turn] * value
                    totals[target] = term if totals[target] is None else totals[target] + term
        return totals

    def own_part(index, carry):
        for member in range(group):
            energy = index * group + member
            for mode in range(modes):
                totals = mix(held, energy, mode, 0, [None] * HALVES)
                for target in range(HALVES):
                    partial[mode, energy, target] = totals[target]
        return carry

    lax.fori_loop(0, energies // group, own_part, 0)

    for turn, part in chunks:
        for side in range(1, cores):
            send_side(turn, part, side).wait_recv()

    def send_out(to_half, to):
        turn = lax.rem(to_half - half + HALVES, HALVES)
        step = lax.rem(to - here + energies, energies)
        return pltpu.make_async_remote_copy(
            src_ref=result.at[to_half, to],
            dst_ref=landed.at[half, here],
            send_sem=out_send.at[turn, step],
            recv_sem=out_recv.at[turn, step],
            device_id=device(to, to_half, core),
            device_id_type=MESH,
        )

    upper = here // reach

    def one_group(index, carry):
        chosen = [
            upper * (group * index + member) + (1 - upper) * (index + member * reach) for member in range(group)
        ]
        sums = [[] for _ in range(modes)]
        for energy in chosen:
            for mode in range(modes):
                totals = [partial[mode, energy, target] for target in range(HALVES)]
                for side in range(1, cores):
                    totals = mix(aside.at[side - 1], energy, mode, side, totals)
                sums[mode].extend(totals)
        rights = []
        for mode in range(modes):
            high, low = split(jnp.concatenate(sums[mode], axis=0))
            rights.append(
                jnp.dot(
                    jnp.concatenate([high, low], axis=1), right_table[mode],
                    preferred_element_type=jnp.float32,
                )
            )
        for member in range(group):
            columns = []
            for target in range(HALVES):
                start = (member * HALVES + target) * rows
                stack = []
                for mode in range(modes):
                    block = rights[mode][start:start + rows]
                    high, low = split(jnp.concatenate([block, pltpu.roll(block, orbitals, 1)], axis=0))
                    stack += [high, low]
                columns.append(jnp.concatenate(stack, axis=0))
            product = jnp.dot(
                left_table[...], jnp.concatenate(columns, axis=1), preferred_element_type=jnp.float32
            )
            energy = chosen[member]
            for target in range(HALVES):
                both = product[:, target * lanes:(target + 1) * lanes]
                result[target, energy] = jnp.where(mask, both[:rows], both[rows:])
                own = jnp.logical_and(energy == here, half == target)

                @pl.when(jnp.logical_not(own))
                def _():
                    send_out(target, energy).start()

        return carry

    lax.fori_loop(0, energies // group, one_group, 0)
    landed[half, here] = result[half, here]

    for step in reversed(far_first):
        for turn in range(HALVES):
            if (turn, step) != (0, 0):
                send_out(around(half, turn, HALVES), around(here, step, energies)).wait_recv()
        pair = around(here, energies - step, energies)
        real, imag = landed[0, pair], landed[1, pair]
        out[0, 0, pair, pl.ds(0, rows), :] = jnp.where(mask, real, pltpu.roll(imag, orbitals, 1))
        out[0, 0, pair, pl.ds(rows, rows), :] = jnp.where(mask, pltpu.roll(real, orbitals, 1), imag)

    for turn, step in slots:
        if (turn, step) != (0, 0):
            send_in(turn, step).wait_send()
            send_out(around(half, turn, HALVES), around(here, step, energies)).wait_send()
    for turn, part in chunks:
        for side in range(1, cores):
            send_side(turn, part, side).wait_send()


def on_device(moms, energies, green_less, couplings, pair_atoms, shift_idx, weights):
    modes, orbitals = couplings.shape[1], couplings.shape[2]
    lanes, rows, cores = 2 * orbitals, orbitals // 2, moms // HALVES
    group = 2
    atoms_first = pair_atoms.T
    modes_first = weights.transpose(1, 0, 2)
    hbm = pl.BlockSpec(memory_space=pl.ANY)
    dma = pltpu.SemaphoreType.DMA
    return pl.pallas_call(
        functools.partial(kernel, (moms, energies, modes, orbitals, group)),
        out_shape=pltpu.VMEM(green_less.shape, jnp.float32),
        in_specs=[hbm] * 5,
        out_specs=pl.BlockSpec(memory_space=pltpu.VMEM),
        scratch_shapes=[
            pltpu.VMEM(green_less.shape, jnp.float32),
            pltpu.VMEM(couplings.shape, jnp.bfloat16),
            pltpu.SMEM(atoms_first.shape, jnp.int32),
            pltpu.SMEM(shift_idx.shape, jnp.int32),
            pltpu.SMEM(modes_first.shape, jnp.float32),
            pltpu.VMEM((HALVES, energies, rows, lanes), jnp.float32),
            pltpu.VMEM((HALVES, energies + 2 * SHIFT_MAX, rows, lanes), jnp.float32),
            pltpu.VMEM((cores - 1, HALVES, energies + 2 * SHIFT_MAX, rows, lanes), jnp.float32),
            pltpu.VMEM((modes, energies, HALVES, rows, lanes), jnp.float32),
            pltpu.VMEM((HALVES, energies, rows, lanes), jnp.float32),
            pltpu.VMEM((HALVES, energies, rows, lanes), jnp.float32),
            pltpu.VMEM((orbitals, modes * lanes), jnp.bfloat16),
            pltpu.VMEM((modes, 2 * lanes, lanes), jnp.bfloat16),
            dma((5,)),
            dma((HALVES, energies)),
            dma((HALVES, energies)),
            dma((cores, HALVES, 4)),
            dma((cores, HALVES, 4)),
            dma((HALVES, energies)),
            dma((HALVES, energies)),
        ],
        compiler_params=pltpu.CompilerParams(
            collective_id=0, has_side_effects=True, vmem_limit_bytes=58 * 2**20
        ),
    )(green_less, couplings, atoms_first, shift_idx, modes_first)


def solution(mesh):
    spec = P("mom", "energy", None, None, None)
    return jax.shard_map(
        functools.partial(on_device, mesh.shape["mom"], mesh.shape["energy"]),
        mesh=mesh,
        in_specs=(spec, P(), P(), P(), P()),
        out_specs=spec,
        check_vma=False,
    )
```

```python
import functools

import jax
import jax.numpy as jnp
from jax import lax
from jax.experimental import pallas as pl
from jax.experimental.pallas import tpu as pltpu
from jax.sharding import PartitionSpec as P

HALVES = 2
SHIFT_MAX = 4
MESH = pl.DeviceIdType.MESH


def split(value):
    high = value.astype(jnp.bfloat16)
    return high, (value - high.astype(jnp.float32)).astype(jnp.bfloat16)


def left_lanes(shape):
    return lax.broadcasted_iota(jnp.int32, shape, len(shape) - 1) < shape[-1] // 2


def iota(shape, axis):
    return lax.broadcasted_iota(jnp.int32, shape, axis)


def kernel(
    sizes,
    green_hbm, couplings_hbm, pair_atoms_hbm, shift_idx_hbm, weights_hbm,
    out,
    green, couplings, pair_atoms, shift_idx, weights, packed, held, aside, partial, result, landed, left_table, right_table,
    load_sem, in_send, in_recv, side_send, side_recv, out_send, out_recv,
):
    moms, energies, modes, orbitals, group = sizes
    reach = energies // 2
    lanes = 2 * orbitals
    rows = orbitals // 2
    cores = moms // HALVES
    here = lax.axis_index("energy")
    mom = lax.axis_index("mom")
    half, core = mom // cores, mom % cores

    def device(at, half_at, core_at):
        return (at, half_at * cores + core_at)

    def around(base, step, size):
        return lax.rem(base + step, size)

    barrier = pltpu.get_barrier_semaphore()
    for turn in range(HALVES):
        for step in range(1 if turn == 0 else 0, energies):
            pl.semaphore_signal(
                barrier, inc=1,
                device_id=device(around(here, step, energies), around(half, turn, HALVES), core),
                device_id_type=MESH,
            )
    for turn in range(1, cores):
        pl.semaphore_signal(
            barrier, inc=1, device_id=device(here, half, around(core, turn, cores)), device_id_type=MESH
        )

    load_green = pltpu.make_async_copy(green_hbm, green, load_sem.at[0])
    load_green.start()
    edge = jnp.zeros((SHIFT_MAX, rows, lanes), jnp.float32)
    for source in range(HALVES):
        held[source, pl.ds(0, SHIFT_MAX)] = edge
        held[source, pl.ds(SHIFT_MAX + energies, SHIFT_MAX)] = edge
        for side in range(1, cores):
            aside[side - 1, source, pl.ds(0, SHIFT_MAX)] = edge
            aside[side - 1, source, pl.ds(SHIFT_MAX + energies, SHIFT_MAX)] = edge

    load_green.wait()
    load_couplings = pltpu.make_async_copy(couplings_hbm, couplings, load_sem.at[1])
    load_couplings.start()
    load_small = [
        pltpu.make_async_copy(pair_atoms_hbm, pair_atoms, load_sem.at[2]),
        pltpu.make_async_copy(shift_idx_hbm, shift_idx, load_sem.at[3]),
        pltpu.make_async_copy(weights_hbm, weights, load_sem.at[4]),
    ]
    for load in load_small:
        load.start()
    mask = left_lanes((rows, lanes))
    for pair in range(energies):
        top = green[0, 0, pair, pl.ds(0, rows), :]
        bottom = green[0, 0, pair, pl.ds(rows, rows), :]
        packed[0, pair] = jnp.where(mask, top, pltpu.roll(bottom, orbitals, 1))
        packed[1, pair] = jnp.where(mask, pltpu.roll(top, orbitals, 1), bottom)

    pl.semaphore_wait(barrier, HALVES * energies - 1 + cores - 1)

    def send_in(turn, step):
        to_half, to = around(half, turn, HALVES), around(here, step, energies)
        return pltpu.make_async_remote_copy(
            src_ref=packed.at[to_half, to],
            dst_ref=held.at[half, SHIFT_MAX + here],
            send_sem=in_send.at[turn, step],
            recv_sem=in_recv.at[turn, here],
            device_id=device(to, to_half, core),
            device_id_type=MESH,
        )

    def send_side(turn, far, side):
        source = around(half, turn, HALVES)
        base = around(here // reach, far, energies // reach) * reach
        block = pl.ds(SHIFT_MAX + base, reach)
        return pltpu.make_async_remote_copy(
            src_ref=held.at[source, block],
            dst_ref=aside.at[side - 1, source, block],
            send_sem=side_send.at[side, turn, far],
            recv_sem=side_recv.at[side, turn, far],
            device_id=device(here, half, around(core, side, cores)),
            device_id_type=MESH,
        )

    def arrive_in(turn, source):
        def wait():
            slot = held.at[around(half, turn, HALVES), SHIFT_MAX + source]
            pltpu.make_async_remote_copy(
                src_ref=slot, dst_ref=slot, send_sem=in_send.at[turn, 0], recv_sem=in_recv.at[turn, source],
                device_id=device(here, half, around(core, 1, cores)), device_id_type=MESH,
            ).wait_recv()

        if turn == 0:
            pl.when(source != here)(wait)
        else:
            wait()

    far_first = sorted(range(energies), key=lambda step: -min(step, energies - step))
    slots = [(turn, step) for step in far_first for turn in range(HALVES)]
    near_first = slots[::-1]
    remote = [slot for slot in slots if slot != (0, 0)]
    for turn, step in remote:
        send_in(turn, step).start()

    held[half, SHIFT_MAX + here] = packed[half, here]

    load_couplings.wait()
    for load in load_small:
        load.wait()
    atom_a = pair_atoms[0, here]
    atom_b = pair_atoms[1, here]
    pick_same = (iota((orbitals, lanes), 0) == iota((orbitals, lanes), 1) % orbitals).astype(jnp.bfloat16)
    pick_other = (
        iota((orbitals, lanes), 0) == (iota((orbitals, lanes), 1) + rows) % orbitals
    ).astype(jnp.bfloat16)
    upper = iota((orbitals, lanes), 0) < rows
    same_block = (iota((lanes, lanes), 0) < orbitals) == (iota((lanes, lanes), 1) < orbitals)
    for mode in range(modes):
        left = couplings[atom_a, mode]
        right = couplings[atom_b, mode]
        left_same = jnp.dot(left, pick_same, preferred_element_type=jnp.float32)
        left_other = jnp.dot(left, pick_other, preferred_element_type=jnp.float32)
        left_table[:, pl.ds(mode * lanes, lanes)] = jnp.where(upper, left_same, left_other).astype(jnp.bfloat16)
        wide = lax.dot_general(
            right, pick_same, (((0,), (0,)), ((), ())), preferred_element_type=jnp.float32
        ).astype(jnp.bfloat16)
        tall = jnp.concatenate([wide, wide], axis=0)
        diagonal = jnp.where(same_block, tall.astype(jnp.float32), 0.0).astype(jnp.bfloat16)
        right_table[mode] = jnp.concatenate([diagonal, diagonal], axis=0)

    chunks = [(turn, far) for far in range(energies // reach) for turn in range(HALVES)]
    for turn, far in chunks:
        base = around(here // reach, far, energies // reach) * reach
        for member in range(reach):
            arrive_in(turn, base + member)
        for side in range(1, cores):
            send_side(turn, far, side).start()
    def mix(block, energy, mode, offset, totals):
        shift = shift_idx[mode]
        for row in range(HALVES):
            source = lax.rem(row + HALVES - (offset > core).astype(jnp.int32), HALVES)
            for sign, slot in ((0, energy - shift), (1, energy + shift)):
                value = block[source, SHIFT_MAX + slot]
                for target in range(HALVES):
                    turn = ((target - row) * cores + offset) % moms
                    term = weights[mode, sign, turn] * value
                    totals[target] = term if totals[target] is None else totals[target] + term
        return totals

    def own_part(index, carry):
        for member in range(group):
            energy = index * group + member
            for mode in range(modes):
                totals = mix(held, energy, mode, 0, [None] * HALVES)
                for target in range(HALVES):
                    partial[mode, energy, target] = totals[target]
        return carry

    lax.fori_loop(0, energies // group, own_part, 0)

    for turn, far in chunks:
        for side in range(1, cores):
            send_side(turn, far, side).wait_recv()

    def send_out(to_half, to):
        turn = lax.rem(to_half - half + HALVES, HALVES)
        step = lax.rem(to - here + energies, energies)
        return pltpu.make_async_remote_copy(
            src_ref=result.at[to_half, to],
            dst_ref=landed.at[half, here],
            send_sem=out_send.at[turn, step],
            recv_sem=out_recv.at[turn, step],
            device_id=device(to, to_half, core),
            device_id_type=MESH,
        )

    upper = here // reach

    def one_group(index, carry):
        chosen = []
        for member in range(group):
            spot = upper * (group * index + member) + (1 - upper) * (index + member * reach)
            late = (spot % reach >= reach // 2).astype(jnp.int32)
            chosen.append(spot + late * (1 - 2 * (spot % 2)))
        sums = [[] for _ in range(modes)]
        for energy in chosen:
            for mode in range(modes):
                totals = [partial[mode, energy, target] for target in range(HALVES)]
                for side in range(1, cores):
                    totals = mix(aside.at[side - 1], energy, mode, side, totals)
                sums[mode].extend(totals)
        rights = []
        for mode in range(modes):
            high, low = split(jnp.concatenate(sums[mode], axis=0))
            rights.append(
                jnp.dot(
                    jnp.concatenate([high, low], axis=1), right_table[mode],
                    preferred_element_type=jnp.float32,
                )
            )
        for member in range(group):
            columns = []
            for target in range(HALVES):
                start = (member * HALVES + target) * rows
                stack = []
                for mode in range(modes):
                    block = rights[mode][start:start + rows]
                    high, low = split(jnp.concatenate([block, pltpu.roll(block, orbitals, 1)], axis=0))
                    stack += [high, low]
                columns.append(jnp.concatenate(stack, axis=0))
            product = jnp.dot(
                left_table[...], jnp.concatenate(columns, axis=1), preferred_element_type=jnp.float32
            )
            energy = chosen[member]
            for target in range(HALVES):
                both = product[:, target * lanes:(target + 1) * lanes]
                result[target, energy] = jnp.where(mask, both[:rows], both[rows:])
                own = jnp.logical_and(energy == here, half == target)

                @pl.when(jnp.logical_not(own))
                def _():
                    send_out(target, energy).start()

        return carry

    lax.fori_loop(0, energies // group, one_group, 0)
    landed[half, here] = result[half, here]

    for step in reversed(far_first):
        for turn in range(HALVES):
            if (turn, step) != (0, 0):
                send_out(around(half, turn, HALVES), around(here, step, energies)).wait_recv()
        pair = around(here, energies - step, energies)
        real, imag = landed[0, pair], landed[1, pair]
        out[0, 0, pair, pl.ds(0, rows), :] = jnp.where(mask, real, pltpu.roll(imag, orbitals, 1))
        out[0, 0, pair, pl.ds(rows, rows), :] = jnp.where(mask, pltpu.roll(real, orbitals, 1), imag)

    for turn, step in slots:
        if (turn, step) != (0, 0):
            send_in(turn, step).wait_send()
            send_out(around(half, turn, HALVES), around(here, step, energies)).wait_send()
    for turn, far in chunks:
        for side in range(1, cores):
            send_side(turn, far, side).wait_send()


def on_device(moms, energies, green_less, couplings, pair_atoms, shift_idx, weights):
    modes, orbitals = couplings.shape[1], couplings.shape[2]
    lanes, rows, cores = 2 * orbitals, orbitals // 2, moms // HALVES
    group = 2
    atoms_first = pair_atoms.T
    modes_first = weights.transpose(1, 0, 2)
    hbm = pl.BlockSpec(memory_space=pl.ANY)
    dma = pltpu.SemaphoreType.DMA
    return pl.pallas_call(
        functools.partial(kernel, (moms, energies, modes, orbitals, group)),
        out_shape=pltpu.VMEM(green_less.shape, jnp.float32),
        in_specs=[hbm] * 5,
        out_specs=pl.BlockSpec(memory_space=pltpu.VMEM),
        scratch_shapes=[
            pltpu.VMEM(green_less.shape, jnp.float32),
            pltpu.VMEM(couplings.shape, jnp.bfloat16),
            pltpu.SMEM(atoms_first.shape, jnp.int32),
            pltpu.SMEM(shift_idx.shape, jnp.int32),
            pltpu.SMEM(modes_first.shape, jnp.float32),
            pltpu.VMEM((HALVES, energies, rows, lanes), jnp.float32),
            pltpu.VMEM((HALVES, energies + 2 * SHIFT_MAX, rows, lanes), jnp.float32),
            pltpu.VMEM((cores - 1, HALVES, energies + 2 * SHIFT_MAX, rows, lanes), jnp.float32),
            pltpu.VMEM((modes, energies, HALVES, rows, lanes), jnp.float32),
            pltpu.VMEM((HALVES, energies, rows, lanes), jnp.float32),
            pltpu.VMEM((HALVES, energies, rows, lanes), jnp.float32),
            pltpu.VMEM((orbitals, modes * lanes), jnp.bfloat16),
            pltpu.VMEM((modes, 2 * lanes, lanes), jnp.bfloat16),
            dma((5,)),
            dma((HALVES, energies)),
            dma((HALVES, energies)),
            dma((cores, HALVES, 2)),
            dma((cores, HALVES, 2)),
            dma((HALVES, energies)),
            dma((HALVES, energies)),
        ],
        compiler_params=pltpu.CompilerParams(
            collective_id=0, has_side_effects=True, vmem_limit_bytes=58 * 2**20
        ),
    )(green_less, couplings, atoms_first, shift_idx, modes_first)


def solution(mesh):
    spec = P("mom", "energy", None, None, None)
    return jax.shard_map(
        functools.partial(on_device, mesh.shape["mom"], mesh.shape["energy"]),
        mesh=mesh,
        in_specs=(spec, P(), P(), P(), P()),
        out_specs=spec,
        check_vma=False,
    )
```
